256 devices in a mesh: img: 8 (over y_lo, x), txt: 32 (over z, y_hi, core).
Axes of the slice: x: 4, y: 4 (y_hi: 2, y_lo: 2; y = y_hi * 2 + y_lo), z: 8, core: 2. Of those that a mesh axis runs over, the one named last changes fastest.
Arguments:
- images: bfloat16 [12288, 1024], P('img'), may hold values from -160 to 160
- texts: bfloat16 [12288, 1024], P('txt'), may hold values from -6 to 6
- match: int32 [12288], P('img'), may hold values from 0 to 12287, each once
Outputs:
- image_grad: float32 [12288, 1024], P(('img', 'txt'))
- text_grad: float32 [12288, 1024], P(('txt', 'img'))
The draws below stay inside these ranges and needn't reach their ends.
Inputs may be any that keep to these rules, and one draw needn't show every extreme that they name: `match`: each text index appears exactly once.
All inputs are finite; a program needn't handle non-finite values.
Results may differ from the reference program's by a relative error of at most 0.0019.
Values may be sent and summed in bfloat16 or wider, within the bound.
No kernel may reach another device: no remote copies, remote signals or barrier semaphores. Data moves between devices by JAX's collectives and lax.ppermute only.
A program may use at most 128 MiB of HBM per device.

```python
import math
import jax
import jax.numpy as jnp
from jax import lax

E = 1024
PAIR_DEV = 48
PAIRS = 12288
N_IMG = 8
N_TXT = 32


def normal_table(key):
    return jnp.clip(jax.random.normal(jax.random.fold_in(key, 11), (PAIRS, E), jnp.float32), -5.5, 5.5)


def aligned_rows(key, table, base, low, high):
    row_ids = jnp.arange(PAIRS, dtype=jnp.int32)
    picked = row_ids % 97 == 5
    first = (row_ids * 7 + 3) % PAIRS
    second = (row_ids * 7 + 4) % PAIRS
    strength = jax.random.uniform(jax.random.fold_in(key, 1), (PAIRS, 1), jnp.float32, low, high)
    factor = strength / (2.0 * math.sqrt(E))
    aligned = factor * (table[first] + table[second])
    values = jnp.where(picked[:, None], aligned, base)
    return jnp.clip(values, -160.0, 160.0)


def draw_texts(key, part):
    values = normal_table(key)
    return values.astype(jnp.bfloat16)


def draw_images(key, part):
    own_key = jax.random.fold_in(key, 3)
    base = jnp.clip(jax.random.normal(own_key, (PAIRS, E), jnp.float32), -5.5, 5.5)
    values = aligned_rows(own_key, normal_table(key), base, 110.0, 220.0)
    return values.astype(jnp.bfloat16)


def setup_inputs(seed: int = 0) -> dict:
    key_list = jax.random.split(jax.random.key(seed), 4)
    images = draw_images(jax.random.fold_in(key_list[3], 71), 0)
    texts = draw_texts(jax.random.fold_in(key_list[3], 71), 0)
    match = jax.random.permutation(key_list[2], PAIRS).astype(jnp.int32)
    return dict(images=images, texts=texts, match=match)


def reference(images, texts, match):
    scale_factor = 2.0 / math.sqrt(E)
    block_rows = PAIR_DEV * N_TXT
    block_cols = PAIR_DEV * N_IMG
    total_rows = images.shape[0]
    image_blocks = images.reshape(total_rows // block_rows, block_rows, E)
    text_blocks = texts.reshape(total_rows // block_cols, block_cols, E)

    def row_spread(image_block):
        logits = jnp.dot(image_block, texts.T, preferred_element_type=jnp.float32) * scale_factor
        highest = lax.optimization_barrier(jnp.max(logits, axis=1))
        return highest + jnp.log(lax.optimization_barrier(jnp.sum(jnp.exp(logits - highest[:, None]), axis=1)))

    def col_spread(text_block):
        logits = jnp.dot(images, text_block.T, preferred_element_type=jnp.float32) * scale_factor
        highest = lax.optimization_barrier(jnp.max(logits, axis=0))
        return highest + jnp.log(lax.optimization_barrier(jnp.sum(jnp.exp(logits - highest[None, :]), axis=0)))
    row_lse = lax.map(row_spread, image_blocks).reshape(total_rows)
    col_lse = lax.map(col_spread, text_blocks).reshape(total_rows)
    column_ids = jnp.arange(total_rows, dtype=jnp.int32)

    def accumulate(running, inputs):
        image_block, match_block, lse_block = inputs
        logits = jnp.dot(image_block, texts.T, preferred_element_type=jnp.float32) * scale_factor
        paired = (match_block[:, None] == column_ids[None, :]).astype(jnp.float32)
        weights = (0.5 * (jnp.exp(logits - lse_block[:, None]) + jnp.exp(logits - col_lse[None, :])) - paired).astype(jnp.bfloat16)
        image_part = jnp.dot(weights, texts, preferred_element_type=jnp.float32)
        running = running + jnp.dot(weights.T, image_block, preferred_element_type=jnp.float32)
        return (running, image_part)
    text_grad, image_parts = lax.scan(accumulate, jnp.zeros((total_rows, E), jnp.float32), (image_blocks, match.reshape(total_rows // block_rows, block_rows), row_lse.reshape(total_rows // block_rows, block_rows)))
    return (image_parts.reshape(total_rows, E), text_grad)
```

```python
import math

import jax
import jax.numpy as jnp
from jax import lax
from jax.sharding import Mesh, PartitionSpec as P

AXES = ("ylo", "x", "z", "yhi", "core")
IMG = ("ylo", "x")
TXT = ("z", "yhi", "core")
F32 = jnp.float32


def swap(value, axis):
    return lax.ppermute(value, axis, [(0, 1), (1, 0)])


def spread(value, axes, n):
    copies = jnp.broadcast_to(value[None], (n,) + value.shape)
    return lax.all_to_all(copies, axes, 0, 0, tiled=True)


def combine(values):
    top = jnp.max(values, axis=0)
    return top + jnp.log(jnp.sum(jnp.exp(values - top[None]), axis=0))


def lse(logits, axis):
    top = jnp.max(logits, axis=axis, keepdims=True)
    return jnp.squeeze(top, axis) + jnp.log(jnp.sum(jnp.exp(logits - top), axis=axis))


def shards(images, texts, match):
    width = images.shape[1]
    scale = 2.0 / math.sqrt(width)
    rows, cols = images.shape[0], texts.shape[0]
    z, yhi, core = (lax.axis_index(a) for a in TXT)
    place = yhi * 2 + core

    other_yhi = swap(texts, "yhi")
    other_core = swap(texts, "core")

    logits = scale * lax.dot_general(
        images, texts, (((1,), (1,)), ((), ())), preferred_element_type=F32
    )
    row_part, col_part = lse(logits, 1), lse(logits, 0)
    row_part = combine(jnp.stack([row_part, swap(row_part, "core")]))
    col_lse = combine(spread(col_part, IMG, 8))
    row_lse = combine(spread(row_part, ("z", "yhi"), 16))

    other_both = swap(other_yhi, "core")
    col_pair = jnp.stack([col_lse, swap(col_lse, "core")])
    col_four = jnp.concatenate([col_pair, swap(col_pair, "yhi")])

    def weigh(logits, row_lse, col_lse, match, ids):
        paired = (match[:, None] == ids[None, :]).astype(F32)
        total = jnp.exp(logits - row_lse[:, None]) + jnp.exp(logits - col_lse[None, :])
        return (0.5 * total - paired).astype(jnp.bfloat16)

    ids = jnp.arange(cols, dtype=jnp.int32)
    weights = weigh(logits, row_lse, col_lse, match, (z * 4 + place) * cols + ids)
    text_part = lax.dot_general(
        weights, images, (((0,), (0,)), ((), ())), preferred_element_type=F32
    ).astype(jnp.bfloat16)
    text_parts = lax.all_to_all(text_part, IMG, 0, 0, tiled=True)
    text_grad = jnp.sum(text_parts.astype(F32).reshape(8, cols // 8, width), axis=0)

    def own(value):
        split = value.reshape((8, 4, rows // 32) + value.shape[1:])
        picked = lax.dynamic_index_in_dim(split, place, 1, keepdims=False)
        return picked.reshape((rows // 4,) + value.shape[1:])

    four = jnp.concatenate([texts, other_core, other_yhi, other_both])
    own_images = own(images)
    own_logits = scale * lax.dot_general(
        own_images, four, (((1,), (1,)), ((), ())), preferred_element_type=F32
    )
    four_ids = jnp.concatenate([(z * 4 + (place ^ k)) * cols + ids for k in range(4)])
    own_weights = weigh(own_logits, own(row_lse), col_four.reshape(-1), own(match), four_ids)
    image_part = jnp.dot(own_weights, four, preferred_element_type=F32).astype(jnp.bfloat16)
    image_parts = lax.all_to_all(image_part, "z", 0, 0, tiled=True)
    image_grad = jnp.sum(image_parts.astype(F32).reshape(8, rows // 32, width), axis=0)
    return image_grad, text_grad


def solution(mesh):
    fine = Mesh(mesh.devices.reshape(2, 4, 8, 2, 2), AXES)
    in_specs = (P(IMG, None), P(TXT, None), P(IMG))
    out_specs = (P(IMG + TXT, None), P(TXT + IMG, None))
    return jax.shard_map(shards, mesh=fine, in_specs=in_specs, out_specs=out_specs, check_vma=False)
```

```python
import functools
import math

import jax
import jax.numpy as jnp
from jax import lax
from jax.experimental import pallas as pl
from jax.experimental.pallas import tpu as pltpu
from jax.sharding import Mesh, PartitionSpec as P

AXES = ("ylo", "x", "z", "yhi", "core")
IMG = ("ylo", "x")
TXT = ("z", "yhi", "core")
F32 = jnp.float32
BF16 = jnp.bfloat16
F16 = jnp.float16
VMEM_LIMIT = 48 * 1024 * 1024
HBM = pl.BlockSpec(memory_space=pl.ANY)
SCALARS = pl.BlockSpec(memory_space=pltpu.SMEM)


def swap(value, axis, bit=1):
    n = {"x": 4}.get(axis, 2)
    return lax.ppermute(value, axis, [(i, i ^ bit) for i in range(n)])


def spread(value, axes, n):
    copies = jnp.broadcast_to(value[None], (n,) + value.shape)
    return lax.all_to_all(copies, axes, 0, 0, tiled=True)


def combine(values, axis):
    top = jnp.max(values, axis=axis, keepdims=True)
    return top + jnp.log(jnp.sum(jnp.exp(values - top), axis=axis, keepdims=True))


def params():
    return pltpu.CompilerParams(vmem_limit_bytes=VMEM_LIMIT)


def nt_dot(a, b):
    return lax.dot_general(a, b, (((1,), (1,)), ((), ())), preferred_element_type=F32)


def first_kernel(scale, steps, text_ref, image_ref, logits_ref, row_ref, col_ref, peak_ref, top_ref, sum_ref):
    step = pl.program_id(0)
    block = image_ref[...]
    logits = nt_dot(text_ref[...], block) * scale
    logits_ref[...] = logits
    row_ref[...] = combine(logits, 0)
    peak = jnp.max(jnp.abs(block).astype(F32), axis=0, keepdims=True)
    peak = jnp.max(peak, axis=1, keepdims=True)
    top = jnp.max(logits, axis=1, keepdims=True)

    @pl.when(step == 0)
    def _():
        top_ref[...] = top
        sum_ref[...] = jnp.sum(jnp.exp(logits - top), axis=1, keepdims=True)
        peak_ref[...] = jnp.broadcast_to(peak, peak_ref.shape)

    @pl.when(step > 0)
    def _():
        old = top_ref[...]
        new = jnp.maximum(old, top)
        total = jnp.sum(jnp.exp(logits - new), axis=1, keepdims=True)
        sum_ref[...] = sum_ref[...] * jnp.exp(old - new) + total
        top_ref[...] = new
        peak_ref[...] = jnp.maximum(peak_ref[...], peak)

    @pl.when(step == steps - 1)
    def _():
        share = top_ref[...] + jnp.log(sum_ref[...])
        col_ref[...] = jnp.transpose(jnp.broadcast_to(share, (share.shape[0], 128)))[:1]


def first_call(texts, images, scale):
    cols, width = texts.shape
    rows = images.shape[0]
    steps = 3
    size = rows // steps
    return pl.pallas_call(
        functools.partial(first_kernel, scale, steps),
        grid=(steps,),
        in_specs=[
            pl.BlockSpec((cols, width), lambda i: (0, 0)),
            pl.BlockSpec((size, width), lambda i: (i, 0)),
        ],
        out_specs=[
            pl.BlockSpec((cols, size), lambda i: (0, i)),
            pl.BlockSpec((1, size), lambda i: (0, i)),
            pl.BlockSpec((1, cols), lambda i: (0, 0)),
            pl.BlockSpec((1, 128), lambda i: (0, 0)),
        ],
        out_shape=[
            jax.ShapeDtypeStruct((cols, rows), F32),
            jax.ShapeDtypeStruct((1, rows), F32),
            jax.ShapeDtypeStruct((1, cols), F32),
            jax.ShapeDtypeStruct((1, 128), F32),
        ],
        scratch_shapes=[pltpu.VMEM((cols, 1), F32), pltpu.VMEM((cols, 1), F32)],
        compiler_params=params(),
        cost_estimate=pl.CostEstimate(
            flops=2 * rows * cols * width, bytes_accessed=6_500_000, transcendentals=2 * rows * cols
        ),
        name="logits",
    )(texts, images)


def weigh(logits, row_lse, col_lse, paired):
    total = jnp.exp(logits - row_lse) + jnp.exp(logits - col_lse)
    return (0.5 * total - paired.astype(F32)).astype(BF16)


def text_kernel(steps, at_ref, logits_ref, row_ref, col_ref, match_ref, image_ref, a_ref, b_ref, c_ref, d_ref, total_ref):
    step = pl.program_id(0)
    cols = logits_ref.shape[0]
    col_lse = jnp.transpose(jnp.broadcast_to(col_ref[...], (128, cols)))[:, :1]
    ids = at_ref[0] + lax.broadcasted_iota(jnp.int32, logits_ref.shape, 0)
    weights = weigh(logits_ref[...], row_ref[...], col_lse, match_ref[...] == ids)
    part = jnp.dot(weights, image_ref[...], preferred_element_type=F32).reshape(total_ref.shape)

    @pl.when(step == 0)
    def _():
        total_ref[...] = part

    @pl.when(step > 0)
    def _():
        total_ref[...] += part

    @pl.when(step == steps - 1)
    def _():
        me = at_ref[1]
        d_ref[...] = total_ref[me]
        c_ref[...] = total_ref[me ^ 1]
        for k in range(2):
            b_ref[k] = total_ref[me ^ (2 + k)]
        for k in range(4):
            a_ref[k] = total_ref[me ^ (4 + k)]


def text_call(at, logits, row_lse, col_lse, match, images):
    cols, rows = logits.shape
    width = images.shape[1]
    steps = 3
    size = rows // steps
    per = cols // 8
    whole = lambda *shape: pl.BlockSpec(shape, lambda i: (0,) * len(shape))
    outs = [(4, per, width), (2, per, width), (per, width), (per, width)]
    return pl.pallas_call(
        functools.partial(text_kernel, steps),
        grid=(steps,),
        in_specs=[
            SCALARS,
            pl.BlockSpec((cols, size), lambda i: (0, i)),
            pl.BlockSpec((1, size), lambda i: (0, i)),
            whole(1, cols),
            pl.BlockSpec((1, size), lambda i: (0, i)),
            pl.BlockSpec((size, width), lambda i: (i, 0)),
        ],
        out_specs=[whole(*s) for s in outs],
        out_shape=[jax.ShapeDtypeStruct(s, F32) for s in outs],
        scratch_shapes=[pltpu.VMEM((8, per, width), F32)],
        compiler_params=params(),
        cost_estimate=pl.CostEstimate(
            flops=2 * rows * cols * width, bytes_accessed=7_000_000, transcendentals=2 * rows * cols
        ),
        name="text_part",
    )(at, logits, row_lse, col_lse, match, images)


def image_kernel(scale, at_ref, row_ref, col_ref, match_ref, image_ref, t0, t1, t2, t3, out_ref, own, four, weights, sems):
    texts = (t0, t1, t2, t3)
    blocks, _, per, width = image_ref.shape
    cols = t0.shape[0]
    place = at_ref[0]
    copies = [pltpu.make_async_copy(image_ref.at[:, place], own, sems.at[4])]
    copies += [
        pltpu.make_async_copy(texts[k], four.at[pl.ds(k * cols, cols)], sems.at[k]) for k in range(4)
    ]
    for copy in copies:
        copy.start()
    rows = blocks * per
    lanes = lax.broadcasted_iota(jnp.int32, (rows, row_ref.shape[1]), 1)
    places = lax.broadcasted_iota(jnp.int32, (rows, row_ref.shape[1]), 0)
    wanted = lanes == places + (places // per) * (3 * per) + place * per
    row_lse = jnp.sum(jnp.where(wanted, row_ref[...], 0.0), axis=1, keepdims=True)
    match = jnp.sum(jnp.where(wanted, match_ref[...], 0), axis=1, keepdims=True)
    copies[0].wait()
    mine = own[...].reshape(rows, width)
    for k in range(4):
        copies[1 + k].wait()
        logits = nt_dot(mine, four[k * cols : (k + 1) * cols]) * scale
        ids = at_ref[1 + k] + lax.broadcasted_iota(jnp.int32, logits.shape, 1)
        weights[:, k * cols : (k + 1) * cols] = weigh(
            logits, row_lse, col_ref[k : k + 1], match == ids
        )
    part = jnp.dot(weights[...], four[...], preferred_element_type=F32)
    out_ref[...] = part.astype(BF16)


def image_call(at, row_lse, col_four, match, images, texts, scale):
    rows, width = images.shape
    cols = texts[0].shape[0]
    own = rows // 4
    full = pl.BlockSpec(memory_space=pltpu.VMEM)
    return pl.pallas_call(
        functools.partial(image_kernel, scale),
        in_specs=[SCALARS, full, full, full] + [HBM] * 5,
        out_specs=full,
        out_shape=jax.ShapeDtypeStruct((own, width), BF16),
        scratch_shapes=[
            pltpu.VMEM((8, rows // 32, width), BF16),
            pltpu.VMEM((4 * cols, width), BF16),
            pltpu.VMEM((own, 4 * cols), BF16),
            pltpu.SemaphoreType.DMA((5,)),
        ],
        compiler_params=params(),
        cost_estimate=pl.CostEstimate(
            flops=4 * own * 4 * cols * width, bytes_accessed=5_000_000, transcendentals=2 * own * 4 * cols
        ),
        name="image_part",
    )(at, row_lse, col_four, match, images.reshape(8, 4, rows // 32, width), *texts)


def shards(images, texts, match):
    rows, width = images.shape
    cols = texts.shape[0]
    scale = 2.0 / math.sqrt(width)
    ylo, x, z, yhi, core = (lax.axis_index(a) for a in AXES)
    place = yhi * 2 + core

    other_yhi = swap(texts, "yhi")
    other_core = swap(texts, "core")

    logits, row_part, col_part, peak = first_call(texts, images, scale)

    sent = jnp.concatenate([row_part, col_part, peak], axis=1)
    got = spread(sent, IMG + ("core",), 16).reshape(8, 2, rows + cols + 128)
    both = lax.dynamic_index_in_dim(got, ylo * 4 + x, 0, keepdims=False)
    row_part = combine(both[:, :rows], 0)
    columns = combine(got[:, :, rows : rows + cols], 0)[0]
    col_lse = lax.dynamic_slice_in_dim(columns, core, 1, 0)
    col_other = lax.dynamic_slice_in_dim(columns, 1 - core, 1, 0)
    peak = jnp.maximum(jnp.max(got[:, :, rows + cols]), 1e-30)
    other_both = swap(other_yhi, "core")

    sent = jnp.concatenate([row_part, col_lse, col_other], axis=1)
    got = spread(sent, ("z", "yhi"), 16)[:, 0]
    row_lse = combine(got[:, :rows], 0)
    across = lax.dynamic_slice_in_dim(got, z * 2 + 1 - yhi, 1, 0)[:, rows:].reshape(2, cols)
    col_four = jnp.concatenate([col_lse, col_other, across])

    bases = jnp.stack([(z * 4 + (place ^ k)) * cols for k in range(4)])
    match = match[None]
    a, b, c, d = text_call(
        jnp.stack([bases[0], ylo * 4 + x]), logits, row_lse, col_lse, match, images
    )
    up, down = 8.0 / peak, peak / 8.0
    a = swap((a * up).astype(F16), "ylo")

    image_part = image_call(
        jnp.concatenate([place[None], bases]), row_lse, col_four, match, images,
        (texts, other_core, other_yhi, other_both), scale,
    )
    image_parts = lax.all_to_all(image_part, "z", 0, 0, tiled=True)
    image_grad = jnp.sum(image_parts.astype(F32).reshape(8, rows // 32, width), axis=0)

    b = swap((b * up + a[2:].astype(F32)).astype(F16), "x", 2)
    c = c * up + a[1].astype(F32)
    d = d * up + a[0].astype(F32)
    c = swap((c + b[1].astype(F32)).astype(F16), "x", 1)
    d = d + b[0].astype(F32)
    text_grad = (d + c.astype(F32)) * down
    return image_grad, text_grad


def solution(mesh):
    fine = Mesh(mesh.devices.reshape(2, 4, 8, 2, 2), AXES)
    in_specs = (P(IMG, None), P(TXT, None), P(IMG))
    out_specs = (P(IMG + TXT, None), P(TXT + IMG, None))
    return jax.shard_map(shards, mesh=fine, in_specs=in_specs, out_specs=out_specs, check_vma=False)
```

```python
import functools
import math

import jax
import jax.numpy as jnp
from jax import lax
from jax.experimental import pallas as pl
from jax.experimental.pallas import tpu as pltpu
from jax.sharding import Mesh, PartitionSpec as P

AXES = ("ylo", "x", "zhi", "zlo", "yhi", "core")
SIZES = (2, 4, 2, 4, 2, 2)
IMG = ("ylo", "x")
TXT = ("zhi", "zlo", "yhi", "core")
F32 = jnp.float32
BF16 = jnp.bfloat16
F16 = jnp.float16
LOG2E = 1.4426950408889634
VMEM_LIMIT = 48 * 1024 * 1024
HBM = pl.BlockSpec(memory_space=pl.ANY)
VMEM = pl.BlockSpec(memory_space=pltpu.VMEM)
SCALARS = pl.BlockSpec(memory_space=pltpu.SMEM)
FREE = pl.CostEstimate(flops=0, bytes_accessed=0, transcendentals=0)
LANES = 128


def swap(value, axis, bit=1):
    n = SIZES[AXES.index(axis)]
    return lax.ppermute(value, axis, [(i, i ^ bit) for i in range(n)])


def z_swap(value, bits):
    pairs = [(z * 2 + c, (z ^ bits[c]) * 2 + c) for z in range(8) for c in range(2)]
    return lax.ppermute(value, ("zhi", "zlo", "core"), pairs)


def img_swap(value, bits):
    pairs = [(i * 2 + c, (i ^ bits[c]) * 2 + c) for i in range(8) for c in range(2)]
    return lax.ppermute(value, ("ylo", "x", "core"), pairs)


def exchange(copies, axes):
    return lax.all_to_all(copies, axes, 0, 0, tiled=True)


def log2_sum(values, axis):
    top = jnp.max(values, axis=axis, keepdims=True)
    return top + jnp.log2(jnp.sum(jnp.exp2(values - top), axis=axis, keepdims=True))


def params():
    return pltpu.CompilerParams(vmem_limit_bytes=VMEM_LIMIT)


def nt_dot(a, b):
    return lax.dot_general(a, b, (((1,), (1,)), ((), ())), preferred_element_type=F32)


def largest(block):
    peak = jnp.max(jnp.abs(block).astype(F32), axis=0, keepdims=True)
    return jnp.max(peak, axis=1, keepdims=True)


def first_kernel(scale, steps, text_ref, image_ref, logits_ref, row_ref, col_ref, top_ref, sum_ref, peak_ref):
    step = pl.program_id(0)
    cols = text_ref.shape[0]
    size = image_ref.shape[0]
    rows = logits_ref.shape[1]
    block = image_ref[...]
    logits = nt_dot(text_ref[...], block) * scale
    where = pl.ds(pl.multiple_of(step * size, size), size)
    logits_ref[:, where] = logits
    row_ref[:, where] = log2_sum(logits, 0)
    peak = largest(block)
    top = jnp.max(logits, axis=1, keepdims=True)

    @pl.when(step == 0)
    def _():
        top_ref[...] = top
        sum_ref[...] = jnp.sum(jnp.exp2(logits - top), axis=1, keepdims=True)
        peak_ref[...] = jnp.broadcast_to(peak, peak_ref.shape)
        row_ref[:, rows:] = jnp.broadcast_to(largest(text_ref[...]), (1, LANES))

    @pl.when(step > 0)
    def _():
        old = top_ref[...]
        new = jnp.maximum(old, top)
        total = jnp.sum(jnp.exp2(logits - new), axis=1, keepdims=True)
        sum_ref[...] = sum_ref[...] * jnp.exp2(old - new) + total
        top_ref[...] = new
        peak_ref[...] = jnp.maximum(peak_ref[...], peak)

    @pl.when(step == steps - 1)
    def _():
        share = top_ref[...] + jnp.log2(sum_ref[...])
        share = jnp.transpose(jnp.broadcast_to(share, (cols, LANES)))[:1]
        for k in range(col_ref.shape[0]):
            col_ref[k, :, :cols] = share
            col_ref[k, :, cols:] = peak_ref[...]


def first_call(texts, images, scale):
    cols, width = texts.shape
    rows = images.shape[0]
    steps = 3
    size = rows // steps
    outs = [(cols, rows), (1, rows + LANES), (8, 1, cols + LANES)]
    return pl.pallas_call(
        functools.partial(first_kernel, scale, steps),
        grid=(steps,),
        in_specs=[
            pl.BlockSpec((cols, width), lambda i: (0, 0)),
            pl.BlockSpec((size, width), lambda i: (i, 0)),
        ],
        out_specs=[pl.BlockSpec(s, lambda i, n=len(s): (0,) * n) for s in outs],
        out_shape=[jax.ShapeDtypeStruct(s, F32) for s in outs],
        scratch_shapes=[
            pltpu.VMEM((cols, 1), F32),
            pltpu.VMEM((cols, 1), F32),
            pltpu.VMEM((1, LANES), F32),
        ],
        compiler_params=params(),
        cost_estimate=FREE,
        name="logits",
    )(texts, images)


def merge_kernel(got_ref, row_ref, cross_ref, out_ref, peak_ref):
    cols = got_ref.shape[2] - LANES
    rows = row_ref.shape[1] - LANES
    got = got_ref[:, 0, :]
    col = log2_sum(got[:, :cols], 0)
    peak_ref[...] = jnp.max(got[:, cols:], axis=0, keepdims=True)
    own, cross = row_ref[...], cross_ref[...]
    top = jnp.maximum(own, cross)
    both = top + jnp.log2(jnp.exp2(own - top) + jnp.exp2(cross - top))
    for k in range(out_ref.shape[0]):
        out_ref[k, :, :rows] = both[:, :rows]
        out_ref[k, :, rows : rows + LANES] = top[:, rows:]
        out_ref[k, :, rows + LANES :] = col


def merge_call(got, row, cross):
    cols = got.shape[2] - LANES
    return pl.pallas_call(
        merge_kernel,
        in_specs=[VMEM] * 3,
        out_specs=[VMEM] * 2,
        out_shape=[
            jax.ShapeDtypeStruct((16, 1, row.shape[1] + cols), F32),
            jax.ShapeDtypeStruct((1, LANES), F32),
        ],
        compiler_params=params(),
        cost_estimate=FREE,
        name="merge",
    )(got, row, cross)


def weigh(logits, row, col, paired):
    total = jnp.exp2(logits - row) + jnp.exp2(logits - col)
    return (0.5 * total - paired.astype(F32)).astype(BF16)


def up_scale(peak):
    return 8.0 / jnp.maximum(peak, 1e-30)


def down_scale(peak):
    return jnp.maximum(peak, 1e-30) * 0.125


def text_kernel(steps, at_ref, logits_ref, stat_ref, peak_ref, match_ref, image_ref, after_ref, out_ref, row_ref, col_ref, total_ref):
    step = pl.program_id(0)
    cols, size = logits_ref.shape
    rows = row_ref.shape[1]

    @pl.when(step == 0)
    def _():
        row_ref[...] = log2_sum(stat_ref[:, 0, :rows], 0)
        col = stat_ref[at_ref[2], :, rows + LANES :]
        col_ref[...] = jnp.transpose(jnp.broadcast_to(col, (LANES, cols)))

    ids = at_ref[0] + lax.broadcasted_iota(jnp.int32, logits_ref.shape, 0)
    row = row_ref[:, pl.ds(pl.multiple_of(step * size, size), size)]
    weights = weigh(logits_ref[...], row, col_ref[:, :1], match_ref[...] == ids)
    part = jnp.dot(weights, image_ref[...], preferred_element_type=F32).reshape(total_ref.shape)

    @pl.when(step == 0)
    def _():
        total_ref[...] = part

    @pl.when(step > 0)
    def _():
        total_ref[...] += part

    @pl.when(step == steps - 1)
    def _():
        out_ref[...] = total_ref[...].astype(BF16)


def put(total, me, core, up, a_ref, b_ref, c_ref, d_ref):
    one, two = 1 + core, 2 - core
    d_ref[...] = total[me] * up
    c_ref[...] = total[me ^ 7] * up
    b_ref[0] = total[me ^ two] * up
    b_ref[1] = total[me ^ two ^ 7] * up
    a_ref[0] = total[me ^ one] * up
    a_ref[1] = total[me ^ one ^ 7] * up
    a_ref[2] = total[me ^ 3] * up
    a_ref[3] = total[me ^ 4] * up


def text_call(at, logits, stats, peak, match, images, after):
    cols, rows = logits.shape
    width = images.shape[1]
    steps = 3
    size = rows // steps
    per = cols // 8
    whole = lambda *shape: pl.BlockSpec(shape, lambda i: (0,) * len(shape))
    outs = [(8, per, width)]
    return pl.pallas_call(
        functools.partial(text_kernel, steps),
        grid=(steps,),
        in_specs=[
            SCALARS,
            pl.BlockSpec((cols, size), lambda i: (0, i)),
            whole(*stats.shape),
            whole(*peak.shape),
            pl.BlockSpec((1, size), lambda i: (0, i)),
            pl.BlockSpec((size, width), lambda i: (i, 0)),
            HBM,
        ],
        out_specs=[whole(*s) for s in outs],
        out_shape=[jax.ShapeDtypeStruct(s, BF16) for s in outs],
        scratch_shapes=[
            pltpu.VMEM((1, rows), F32),
            pltpu.VMEM((cols, LANES), F32),
            pltpu.VMEM((8, per, width), F32),
        ],
        compiler_params=params(),
        cost_estimate=FREE,
        name="text_part",
    )(at, logits, stats, peak, match, images, after)[0]


def image_kernel(scale, at_ref, stat_ref, match_ref, image_ref, t0, t1, t2, t3, a_ref, b_ref, c_ref, d_ref, own, four, weights, total, sems):
    texts = (t0, t1, t2, t3)
    blocks, _, per, width = image_ref.shape
    cols = t0.shape[0]
    place, z, core = at_ref[0], at_ref[5], at_ref[6]
    copies = [pltpu.make_async_copy(image_ref.at[:, place], own, sems.at[4])]
    copies += [
        pltpu.make_async_copy(texts[k], four.at[pl.ds(k * cols, cols)], sems.at[k]) for k in range(4)
    ]
    for copy in copies:
        copy.start()
    rows = blocks * per
    every = match_ref.shape[1]
    lanes = lax.broadcasted_iota(jnp.int32, (rows, every), 1)
    places = lax.broadcasted_iota(jnp.int32, (rows, every), 0)
    wanted = lanes == places + (places // per) * (3 * per) + place * per
    row = log2_sum(stat_ref[:, 0, :every], 0)
    row = jnp.sum(jnp.where(wanted, row, 0.0), axis=1, keepdims=True)
    match = jnp.sum(jnp.where(wanted, match_ref[...], 0), axis=1, keepdims=True)
    copies[0].wait()
    mine = own[...].reshape(rows, width)
    first = (z % 4) * 4
    for k in range(4):
        copies[1 + k].wait()
        logits = nt_dot(mine, four[k * cols : (k + 1) * cols]) * scale
        ids = at_ref[1 + k] + lax.broadcasted_iota(jnp.int32, logits.shape, 1)
        col = stat_ref[first + (place ^ k), :, every + LANES :]
        weights[:, k * cols : (k + 1) * cols] = weigh(logits, row, col, match == ids)
    part = jnp.dot(weights[...], four[...], preferred_element_type=F32)
    peak = jnp.max(stat_ref[:, 0, every : every + LANES])
    total[...] = part.reshape(total.shape)
    put(total, z, core, up_scale(peak), a_ref, b_ref, c_ref, d_ref)


def image_call(at, stats, match, images, texts, scale):
    rows, width = images.shape
    cols = texts[0].shape[0]
    own = rows // 4
    per = rows // 32
    outs = [(4, per, width), (2, per, width), (per, width), (per, width)]
    return pl.pallas_call(
        functools.partial(image_kernel, scale),
        in_specs=[SCALARS, VMEM, VMEM] + [HBM] * 5,
        out_specs=[VMEM] * 4,
        out_shape=[jax.ShapeDtypeStruct(s, F32) for s in outs],
        scratch_shapes=[
            pltpu.VMEM((8, per, width), BF16),
            pltpu.VMEM((4 * cols, width), BF16),
            pltpu.VMEM((own, 4 * cols), BF16),
            pltpu.VMEM((8, per, width), F32),
            pltpu.SemaphoreType.DMA((5,)),
        ],
        compiler_params=params(),
        cost_estimate=FREE,
        name="image_part",
    )(at, stats, match, images.reshape(8, 4, per, width), *texts)


def halve(parts, swap_by):
    a, b, c, d = parts
    a = swap_by(a.astype(F16), (1, 2))
    b = swap_by((b + a[2:].astype(F32)).astype(F16), (2, 1))
    c = c + a[1].astype(F32)
    d = d + a[0].astype(F32)
    c = swap_by((c + b[1].astype(F32)).astype(F16), (7, 7))
    return d + b[0].astype(F32) + c.astype(F32)


def shards(images, texts, match):
    rows, width = images.shape
    cols = texts.shape[0]
    scale = 2.0 / math.sqrt(width) * LOG2E
    ylo, x, zhi, zlo, yhi, core = (lax.axis_index(a) for a in AXES)
    place = yhi * 2 + core
    z = zhi * 4 + zlo

    other_yhi = swap(texts, "yhi")
    other_core = swap(texts, "core")

    logits, row, col = first_call(texts, images, scale)
    cross = z_swap(row, (7, 7))
    got = exchange(col, IMG)
    sent, image_peak = merge_call(got, row, cross)
    other_yhi, sent = lax.optimization_barrier((other_yhi, sent))
    stats = exchange(sent, ("zlo", "yhi", "core"))
    other_both = swap(other_yhi, "core")

    bases = jnp.stack([(z * 4 + (place ^ k)) * cols for k in range(4)])
    match = match[None]
    image_parts = image_call(
        jnp.concatenate([place[None], bases, z[None], core[None]]), stats, match, images,
        (texts, other_core, other_yhi, other_both), scale,
    )
    text_parts = text_call(
        jnp.stack([bases[0], ylo * 4 + x, zlo * 4 + place, core]), logits, stats, image_peak, match, images,
        image_parts[3],
    )
    image_grad = halve(image_parts, z_swap)
    text_grad = jnp.sum(exchange(text_parts, IMG).astype(F32), axis=0)
    text_peak = jnp.max(stats[:, 0, rows : rows + 1])
    return image_grad * down_scale(text_peak), text_grad


def solution(mesh):
    fine = Mesh(mesh.devices.reshape(SIZES), AXES)
    in_specs = (P(IMG, None), P(TXT, None), P(IMG))
    out_specs = (P(IMG + TXT, None), P(TXT + IMG, None))
    return jax.shard_map(shards, mesh=fine, in_specs=in_specs, out_specs=out_specs, check_vma=False)
```

```python
import functools
import math

import jax
import jax.numpy as jnp
from jax import lax
from jax.experimental import pallas as pl
from jax.experimental.pallas import tpu as pltpu
from jax.sharding import Mesh, PartitionSpec as P

AXES = ("ylo", "x", "zhi", "zb", "za", "yhi", "core")
SIZES = (2, 4, 2, 2, 2, 2, 2)
IMG = ("ylo", "x")
TXT = ("zhi", "zb", "za", "yhi", "core")
F32 = jnp.float32
BF16 = jnp.bfloat16
F16 = jnp.float16
LOG2E = 1.4426950408889634
HBM = pl.BlockSpec(memory_space=pltpu.HBM)
VMEM = pl.BlockSpec(memory_space=pltpu.VMEM)
SCALARS = pl.BlockSpec(memory_space=pltpu.SMEM)
FREE = pl.CostEstimate(flops=0, bytes_accessed=0, transcendentals=0)
LANES = 128
MIB = 1024 * 1024


def swap(value, axis):
    return lax.ppermute(value, axis, [(0, 1), (1, 0)])


def z_swap(value, bits):
    pairs = [(z * 2 + c, (z ^ bits[c]) * 2 + c) for z in range(8) for c in range(2)]
    return lax.ppermute(value, ("zhi", "zb", "za", "core"), pairs)


def exchange(copies, axes):
    return lax.all_to_all(copies, axes, 0, 0, tiled=True)


def tie(*values):
    return lax.optimization_barrier(values)


def log2_sum(values, axis):
    top = jnp.max(values, axis=axis, keepdims=True)
    return top + jnp.log2(jnp.sum(jnp.exp2(values - top), axis=axis, keepdims=True))


def merge(own, got, n):
    top = jnp.maximum(own, got)
    total = top + jnp.log2(jnp.exp2(own - top) + jnp.exp2(got - top))
    lanes = lax.broadcasted_iota(jnp.int32, own.shape, 1)
    return jnp.where(lanes < n, total, top)


def params(mib):
    return pltpu.CompilerParams(vmem_limit_bytes=mib * MIB)


def nt_dot(a, b):
    return lax.dot_general(a, b, (((1,), (1,)), ((), ())), preferred_element_type=F32)


def largest(block):
    peak = jnp.max(jnp.abs(block).astype(F32), axis=0, keepdims=True)
    return jnp.max(peak, axis=1, keepdims=True)


def first_kernel(scale, text_in, image_in, logits_out, row_ref, col_ref, text_ref, image_ref, logits_ref, sems):
    cols = text_in.shape[0]
    rows = image_in.shape[0]
    size = rows // 3
    steps = range(0, rows, size)
    fetch = [pltpu.make_async_copy(text_in, text_ref, sems.at[0])]
    fetch += [
        pltpu.make_async_copy(image_in.at[pl.ds(j, size)], image_ref.at[pl.ds(j, size)], sems.at[1 + k])
        for k, j in enumerate(steps)
    ]
    for copy in fetch:
        copy.start()
    fetch[0].wait()
    text = text_ref[...]
    row_ref[:, rows:] = jnp.broadcast_to(largest(text), (1, LANES))
    high = total = None
    store = []
    for k, j in enumerate(steps):
        fetch[1 + k].wait()
        logits = nt_dot(text, image_ref[j : j + size]) * scale
        logits_ref[:, j : j + size] = logits
        where = pl.ds(j, size)
        store.append(pltpu.make_async_copy(logits_ref.at[:, where], logits_out.at[:, where], sems.at[4 + k]))
        store[k].start()
        deep = logits.reshape(cols // 8, 8, size)
        top = jnp.max(deep, axis=0)
        part = jnp.sum(jnp.exp2(deep - top[None]), axis=0)
        best = jnp.max(top, axis=0, keepdims=True)
        part = jnp.sum(part * jnp.exp2(top - best), axis=0, keepdims=True)
        row_ref[:, j : j + size] = best + jnp.log2(part)
        tiles = [logits[:, i : i + LANES] for i in range(0, size, LANES)]
        new = functools.reduce(jnp.maximum, tiles if high is None else [high, *tiles])
        sums = [jnp.exp2(tile - new) for tile in tiles]
        total = functools.reduce(jnp.add, sums if high is None else [total * jnp.exp2(high - new), *sums])
        high = new
    best = jnp.max(high, axis=1, keepdims=True)
    share = best + jnp.log2(jnp.sum(total * jnp.exp2(high - best), axis=1, keepdims=True))
    share = jnp.transpose(jnp.broadcast_to(share, (cols, LANES)))[:1]
    for k in range(col_ref.shape[0]):
        col_ref[k] = share
    for copy in store:
        copy.wait()


def first_call(texts, images, scale):
    cols = texts.shape[0]
    rows = images.shape[0]
    outs = [(cols, rows), (1, rows + LANES), (8, 1, cols)]
    return pl.pallas_call(
        functools.partial(first_kernel, scale),
        in_specs=[HBM] * 2,
        out_specs=[HBM, VMEM, VMEM],
        out_shape=[jax.ShapeDtypeStruct(s, F32) for s in outs],
        scratch_shapes=[
            pltpu.VMEM(texts.shape, BF16),
            pltpu.VMEM(images.shape, BF16),
            pltpu.VMEM((cols, rows), F32),
            pltpu.SemaphoreType.DMA((7,)),
        ],
        compiler_params=params(60),
        cost_estimate=FREE,
        name="logits",
    )(texts, images)


def merge_kernel(got_ref, row_ref, near_ref, out_ref):
    rows = row_ref.shape[1]
    col = log2_sum(got_ref[:, 0, :], 0)
    both = merge(row_ref[...], near_ref[...], rows - LANES)
    for k in range(out_ref.shape[0]):
        out_ref[k, :, :rows] = both
        out_ref[k, :, rows:] = col


def merge_call(got, row, near):
    cols = got.shape[2]
    return pl.pallas_call(
        merge_kernel,
        in_specs=[VMEM] * 3,
        out_specs=VMEM,
        out_shape=jax.ShapeDtypeStruct((8, 1, row.shape[1] + cols), F32),
        compiler_params=params(4),
        cost_estimate=FREE,
        name="merge",
    )(got, row, near)


def weigh(logits, row, col, paired):
    total = jnp.exp2(logits - row) + jnp.exp2(logits - col)
    return (0.5 * total - paired.astype(F32)).astype(BF16)


def up_scale(peak):
    return 8.0 / jnp.maximum(peak, 1e-30)


def down_scale(peak):
    return jnp.maximum(peak, 1e-30) * 0.125


def text_kernel(at_ref, logits_in, stat_ref, match_ref, image_in, after_ref, out_ref, logits_ref, image_ref, weights, sems):
    cols, rows = logits_in.shape
    size = rows // 4
    steps = range(0, rows, size)
    fetch = [
        pltpu.make_async_copy(logits_in.at[:, pl.ds(j, size)], logits_ref.at[:, pl.ds(j, size)], sems.at[k])
        for k, j in enumerate(steps)
    ]
    fetch.append(pltpu.make_async_copy(image_in, image_ref, sems.at[4]))
    for copy in fetch:
        copy.start()
    row = log2_sum(stat_ref[:, 0, :rows], 0)
    col = stat_ref[at_ref[7] + at_ref[0], :, rows + LANES :]
    col = jnp.transpose(jnp.broadcast_to(col, (LANES, cols)))[:, :1]
    ids = at_ref[1] + lax.broadcasted_iota(jnp.int32, (cols, size), 0)
    for k, j in enumerate(steps):
        fetch[k].wait()
        paired = match_ref[:, j : j + size] == ids
        weights[:, j : j + size] = weigh(logits_ref[:, j : j + size], row[:, j : j + size], col, paired)
    fetch[4].wait()
    part = jnp.dot(weights[...], image_ref[...], preferred_element_type=F32)
    out_ref[...] = part.astype(BF16).reshape(out_ref.shape)


def text_call(at, logits, stats, match, images, after):
    cols, rows = logits.shape
    width = images.shape[1]
    return pl.pallas_call(
        text_kernel,
        in_specs=[SCALARS, HBM, VMEM, VMEM, HBM, HBM],
        out_specs=VMEM,
        out_shape=jax.ShapeDtypeStruct((8, cols // 8, width), BF16),
        scratch_shapes=[
            pltpu.VMEM((cols, rows), F32),
            pltpu.VMEM(images.shape, BF16),
            pltpu.VMEM((cols, rows), BF16),
            pltpu.SemaphoreType.DMA((5,)),
        ],
        compiler_params=params(60),
        cost_estimate=FREE,
        name="text_part",
    )(at, logits, stats, match, images, after)


def image_kernel(scale, at_ref, stat_ref, match_ref, image_ref, t0, t1, t2, t3, a_ref, b_ref, c_ref, d_ref, down_ref, own, four, row_all, weights, sems):
    texts = (t0, t1, t2, t3)
    blocks, _, per, width = image_ref.shape
    cols = t0.shape[0]
    rows = blocks * per
    every = match_ref.shape[1]
    place, z, core, first = at_ref[0], at_ref[5], at_ref[6], at_ref[7]
    one, two = 1 + core, 2 - core
    order = [z ^ one, z ^ one ^ 7, z ^ 3, z ^ 4, z ^ two, z ^ two ^ 7, z ^ 7, z]
    fetch = [
        pltpu.make_async_copy(image_ref.at[block, place], own.at[k], sems.at[4]) for k, block in enumerate(order)
    ]
    fetch += [
        pltpu.make_async_copy(texts[k], four.at[pl.ds(k * cols, cols)], sems.at[k]) for k in range(4)
    ]
    for copy in fetch:
        copy.start()
    row_all[...] = log2_sum(stat_ref[:, 0, :every], 0)
    span = 2 * LANES
    lanes = lax.broadcasted_iota(jnp.int32, (per, span), 1) - lax.broadcasted_iota(jnp.int32, (per, span), 0)
    row, match = [], []
    for block in order:
        begin = block * (4 * per) + place * per
        start = jnp.minimum(begin // LANES * LANES, every - span)
        window = pl.ds(pl.multiple_of(start, LANES), span)
        wanted = lanes == begin - start
        row.append(jnp.sum(jnp.where(wanted, row_all[:, window], 0.0), axis=1, keepdims=True))
        match.append(jnp.sum(jnp.where(wanted, match_ref[:, window], 0), axis=1, keepdims=True))
    row = jnp.concatenate(row, axis=0)
    match = jnp.concatenate(match, axis=0)
    ids = lax.broadcasted_iota(jnp.int32, (rows, cols), 1)
    for copy in fetch[:8]:
        copy.wait()
    mine = own[...].reshape(rows, width)
    for k in range(4):
        fetch[8 + k].wait()
        where = slice(k * cols, (k + 1) * cols)
        logits = nt_dot(mine, four[where]) * scale
        col = stat_ref[first + (place ^ k), :, every + LANES :]
        weights[:, where] = weigh(logits, row, col, match - at_ref[1 + k] == ids)
    peak = jnp.max(stat_ref[:, 0, every : every + LANES], axis=0, keepdims=True)
    down_ref[...] = down_scale(peak)
    part = jnp.dot(weights[...], four[...], preferred_element_type=F32) * up_scale(peak[:, :1])
    a_ref[...] = part[: 4 * per].astype(a_ref.dtype).reshape(a_ref.shape)
    b_ref[...] = part[4 * per : 6 * per].reshape(b_ref.shape)
    c_ref[...] = part[6 * per : 7 * per]
    d_ref[...] = part[7 * per :]


def image_call(at, stats, match, images, texts, scale):
    rows, width = images.shape
    cols = texts[0].shape[0]
    own = rows // 4
    per = rows // 32
    outs = [(4, per, width), (2, per, width), (per, width), (per, width), (1, LANES)]
    kinds = [BF16, F32, F32, F32, F32]
    return pl.pallas_call(
        functools.partial(image_kernel, scale),
        in_specs=[SCALARS, VMEM, VMEM] + [HBM] * 5,
        out_specs=[VMEM] * 5,
        out_shape=[jax.ShapeDtypeStruct(s, t) for s, t in zip(outs, kinds)],
        scratch_shapes=[
            pltpu.VMEM((8, per, width), BF16),
            pltpu.VMEM((4 * cols, width), BF16),
            pltpu.VMEM((1, rows), F32),
            pltpu.VMEM((own, 4 * cols), BF16),
            pltpu.SemaphoreType.DMA((5,)),
        ],
        compiler_params=params(60),
        cost_estimate=FREE,
        name="image_part",
    )(at, stats, match, images.reshape(8, 4, per, width), *texts)


def shards(images, texts, match):
    rows, width = images.shape
    cols = texts.shape[0]
    scale = 2.0 / math.sqrt(width) * LOG2E
    zhi, zb, za, yhi, core = (lax.axis_index(a) for a in TXT)
    place = yhi * 2 + core
    z = zhi * 4 + zb * 2 + za

    other_yhi = swap(texts, "yhi")
    other_core = swap(texts, "core")

    logits, row, col = first_call(texts, images, scale)
    cross = z_swap(row, (7, 7))
    row = merge(row, cross, rows)
    near = z_swap(row, (1, 1))
    got = exchange(col, IMG)
    sent = merge_call(got, row, near)
    other_yhi, sent = tie(other_yhi, sent)
    stats = exchange(sent, ("zb", "yhi", "core"))
    other_both = swap(other_yhi, "core")

    bases = [(z * 4 + (place ^ k)) * cols for k in range(4)]
    at = jnp.stack([place, *bases, z, core, zb * 4])
    match = match[None]
    a, b, c, d, down = image_call(at, stats, match, images, (texts, other_core, other_yhi, other_both), scale)
    text_parts = text_call(at, logits, stats, match, images, d)

    a = z_swap(a, (1, 2))
    b = (b + a[2:].astype(F32)).astype(F16)
    b = z_swap(b, (2, 1))
    c = c + a[1].astype(F32)
    d = d + a[0].astype(F32)
    text_parts = exchange(text_parts, IMG)
    b, c, d = tie(b, c, d)
    c = z_swap((c + b[1].astype(F32)).astype(F16), (7, 7))
    d = d + b[0].astype(F32)
    text_grad = jnp.sum(text_parts.astype(F32), axis=0)
    c, d = tie(c, d)
    return (d + c.astype(F32)) * down[:, :1], text_grad


def solution(mesh):
    fine = Mesh(mesh.devices.reshape(SIZES), AXES)
    in_specs = (P(IMG, None), P(TXT, None), P(IMG))
    out_specs = (P(IMG + TXT, None), P(TXT + IMG, None))
    return jax.shard_map(shards, mesh=fine, in_specs=in_specs, out_specs=out_specs, check_vma=False)
```

```python
import functools
import math

import jax
import jax.numpy as jnp
from jax import lax
from jax.experimental import pallas as pl
from jax.experimental.pallas import tpu as pltpu
from jax.sharding import Mesh, PartitionSpec as P

AXES = ("ylo", "x", "zhi", "zb", "za", "yhi", "core")
SIZES = (2, 4, 2, 2, 2, 2, 2)
IMG = ("ylo", "x")
TXT = ("zhi", "zb", "za", "yhi", "core")
F32 = jnp.float32
BF16 = jnp.bfloat16
F16 = jnp.float16
LOG2E = 1.4426950408889634
HBM = pl.BlockSpec(memory_space=pltpu.HBM)
VMEM = pl.BlockSpec(memory_space=pltpu.VMEM)
SCALARS = pl.BlockSpec(memory_space=pltpu.SMEM)
FREE = pl.CostEstimate(flops=0, bytes_accessed=0, transcendentals=0)
LANES = 128
MIB = 1024 * 1024


def swap(value, axis):
    return lax.ppermute(value, axis, [(0, 1), (1, 0)])


def z_swap(value, bits):
    pairs = [(z * 2 + c, (z ^ bits[c]) * 2 + c) for z in range(8) for c in range(2)]
    return lax.ppermute(value, ("zhi", "zb", "za", "core"), pairs)


def exchange(copies, axes):
    return lax.all_to_all(copies, axes, 0, 0, tiled=True)


def tie(*values):
    return lax.optimization_barrier(values)


def log2_sum(values, axis):
    top = jnp.max(values, axis=axis, keepdims=True)
    return top + jnp.log2(jnp.sum(jnp.exp2(values - top), axis=axis, keepdims=True))


def merge(own, got, n):
    top = jnp.maximum(own, got)
    total = top + jnp.log2(jnp.exp2(own - top) + jnp.exp2(got - top))
    lanes = lax.broadcasted_iota(jnp.int32, own.shape, 1)
    return jnp.where(lanes < n, total, top)


def params(mib):
    return pltpu.CompilerParams(vmem_limit_bytes=mib * MIB)


def nt_dot(a, b):
    return lax.dot_general(a, b, (((1,), (1,)), ((), ())), preferred_element_type=F32)


def largest(block):
    peak = jnp.max(jnp.abs(block).astype(F32), axis=0, keepdims=True)
    return jnp.max(peak, axis=1, keepdims=True)


def first_kernel(scale, text_in, image_in, logits_out, row_ref, col_ref, text_ref, image_ref, logits_ref, sems):
    cols = text_in.shape[0]
    rows = image_in.shape[0]
    size = rows // 3
    steps = range(0, rows, size)
    fetch = [pltpu.make_async_copy(text_in, text_ref, sems.at[0])]
    fetch += [
        pltpu.make_async_copy(image_in.at[pl.ds(j, size)], image_ref.at[pl.ds(j, size)], sems.at[1 + k])
        for k, j in enumerate(steps)
    ]
    for copy in fetch:
        copy.start()
    fetch[0].wait()
    text = text_ref[...]
    row_ref[:, rows:] = jnp.broadcast_to(largest(text), (1, LANES))
    high = total = None
    store = []
    for k in range(len(steps) + 1):
        if k < len(steps):
            fetch[1 + k].wait()
            where = pl.ds(steps[k], size)
            logits_ref[:, where] = nt_dot(text, image_ref[where]) * scale
            store.append(pltpu.make_async_copy(logits_ref.at[:, where], logits_out.at[:, where], sems.at[4 + k]))
            store[k].start()
        if k == 0:
            continue
        j = steps[k - 1]
        logits = logits_ref[:, j : j + size]
        deep = logits.reshape(cols // 8, 8, size)
        top = jnp.max(deep, axis=0)
        part = jnp.sum(jnp.exp2(deep - top[None]), axis=0)
        best = jnp.max(top, axis=0, keepdims=True)
        part = jnp.sum(part * jnp.exp2(top - best), axis=0, keepdims=True)
        row_ref[:, j : j + size] = best + jnp.log2(part)
        tiles = [logits[:, i : i + LANES] for i in range(0, size, LANES)]
        new = functools.reduce(jnp.maximum, tiles if high is None else [high, *tiles])
        sums = [jnp.exp2(tile - new) for tile in tiles]
        total = functools.reduce(jnp.add, sums if high is None else [total * jnp.exp2(high - new), *sums])
        high = new
    best = jnp.max(high, axis=1, keepdims=True)
    share = best + jnp.log2(jnp.sum(total * jnp.exp2(high - best), axis=1, keepdims=True))
    share = jnp.transpose(jnp.broadcast_to(share, (cols, LANES)))[:1]
    for k in range(col_ref.shape[0]):
        col_ref[k] = share
    for copy in store:
        copy.wait()


def first_call(texts, images, scale):
    cols = texts.shape[0]
    rows = images.shape[0]
    outs = [(cols, rows), (1, rows + LANES), (8, 1, cols)]
    return pl.pallas_call(
        functools.partial(first_kernel, scale),
        in_specs=[HBM] * 2,
        out_specs=[HBM, VMEM, VMEM],
        out_shape=[jax.ShapeDtypeStruct(s, F32) for s in outs],
        scratch_shapes=[
            pltpu.VMEM(texts.shape, BF16),
            pltpu.VMEM(images.shape, BF16),
            pltpu.VMEM((cols, rows), F32),
            pltpu.SemaphoreType.DMA((7,)),
        ],
        compiler_params=params(60),
        cost_estimate=FREE,
        name="logits",
    )(texts, images)


def merge_kernel(got_ref, row_ref, near_ref, out_ref):
    rows = row_ref.shape[1]
    col = log2_sum(got_ref[:, 0, :], 0)
    both = merge(row_ref[...], near_ref[...], rows - LANES)
    for k in range(out_ref.shape[0]):
        out_ref[k, :, :rows] = both
        out_ref[k, :, rows:] = col


def merge_call(got, row, near):
    cols = got.shape[2]
    return pl.pallas_call(
        merge_kernel,
        in_specs=[VMEM] * 3,
        out_specs=VMEM,
        out_shape=jax.ShapeDtypeStruct((8, 1, row.shape[1] + cols), F32),
        compiler_params=params(4),
        cost_estimate=FREE,
        name="merge",
    )(got, row, near)


def weigh(logits, row, col, paired):
    total = jnp.exp2(logits - row) + jnp.exp2(logits - col)
    return (0.5 * total - paired.astype(F32)).astype(BF16)


def up_scale(peak):
    return 8.0 / jnp.maximum(peak, 1e-30)


def down_scale(peak):
    return jnp.maximum(peak, 1e-30) * 0.125


def text_kernel(at_ref, logits_in, stat_in, match_in, image_in, after_ref, out_ref, stat_ref, match_ref, logits_ref, image_ref, weights, sems):
    cols, rows = logits_in.shape
    size = rows // 4
    steps = range(0, rows, size)
    fetch = [
        pltpu.make_async_copy(logits_in.at[:, pl.ds(j, size)], logits_ref.at[:, pl.ds(j, size)], sems.at[k])
        for k, j in enumerate(steps)
    ]
    fetch.append(pltpu.make_async_copy(image_in, image_ref, sems.at[4]))
    facts = [pltpu.make_async_copy(stat_in, stat_ref, sems.at[5]), pltpu.make_async_copy(match_in, match_ref, sems.at[6])]
    for copy in facts + fetch:
        copy.start()
    for copy in facts:
        copy.wait()
    row = log2_sum(stat_ref[:, 0, :rows], 0)
    col = stat_ref[at_ref[7] + at_ref[0], :, rows + LANES :]
    col = jnp.transpose(jnp.broadcast_to(col, (LANES, cols)))[:, :1]
    ids = at_ref[1] + lax.broadcasted_iota(jnp.int32, (cols, size), 0)
    for k, j in enumerate(steps):
        fetch[k].wait()
        paired = match_ref[:, j : j + size] == ids
        weights[:, j : j + size] = weigh(logits_ref[:, j : j + size], row[:, j : j + size], col, paired)
    fetch[4].wait()
    part = jnp.dot(weights[...], image_ref[...], preferred_element_type=F32)
    out_ref[...] = part.astype(BF16).reshape(out_ref.shape)


def text_call(at, logits, stats, match, images, after):
    cols, rows = logits.shape
    width = images.shape[1]
    return pl.pallas_call(
        text_kernel,
        in_specs=[SCALARS] + [HBM] * 5,
        out_specs=VMEM,
        out_shape=jax.ShapeDtypeStruct((8, cols // 8, width), BF16),
        scratch_shapes=[
            pltpu.VMEM(stats.shape, F32),
            pltpu.VMEM(match.shape, jnp.int32),
            pltpu.VMEM((cols, rows), F32),
            pltpu.VMEM(images.shape, BF16),
            pltpu.VMEM((cols, rows), BF16),
            pltpu.SemaphoreType.DMA((7,)),
        ],
        compiler_params=params(60),
        cost_estimate=FREE,
        name="text_part",
    )(at, logits, stats, match, images, after)


def image_kernel(scale, at_ref, stat_in, match_in, image_ref, t0, t1, t2, t3, a_ref, b_ref, c_ref, d_ref, down_ref, stat_ref, match_ref, own, four, row_by, match_by, weights, sems):
    texts = (t0, t1, t2, t3)
    blocks, _, per, width = image_ref.shape
    cols = t0.shape[0]
    rows = blocks * per
    every = match_in.shape[1]
    place, z, core, first = at_ref[0], at_ref[5], at_ref[6], at_ref[7]
    one, two = 1 + core, 2 - core
    order = [z ^ one, z ^ one ^ 7, z ^ 3, z ^ 4, z ^ two, z ^ two ^ 7, z ^ 7, z]
    fetch = [
        pltpu.make_async_copy(stat_in, stat_ref, sems.at[5]),
        pltpu.make_async_copy(match_in, match_ref, sems.at[6]),
    ]
    fetch += [
        pltpu.make_async_copy(image_ref.at[block, place], own.at[k], sems.at[4]) for k, block in enumerate(order)
    ]
    fetch += [
        pltpu.make_async_copy(texts[k], four.at[pl.ds(k * cols, cols)], sems.at[k]) for k in range(4)
    ]
    for copy in fetch:
        copy.start()
    fetch[0].wait()
    fetch[1].wait()
    row_all = log2_sum(stat_ref[:, 0, :every], 0)
    pair = lax.broadcasted_iota(jnp.int32, (2 * per, 1), 0)
    lane = pair + jnp.where(pair < per, 0, 3 * per) + place * per
    wanted = lax.broadcasted_iota(jnp.int32, (2 * per, 8 * per), 1) == lane
    for k, j in enumerate(range(0, every, 8 * per)):
        window = slice(j, j + 8 * per)
        row = jnp.sum(jnp.where(wanted, row_all[:, window], 0.0), axis=1, keepdims=True)
        match = jnp.sum(jnp.where(wanted, match_ref[:, window], 0), axis=1, keepdims=True)
        row_by[2 * k : 2 * k + 2] = row.reshape(2, per, 1)
        match_by[2 * k : 2 * k + 2] = match.reshape(2, per, 1)
    row = jnp.concatenate([row_by[block] for block in order], axis=0)
    match = jnp.concatenate([match_by[block] for block in order], axis=0)
    ids = lax.broadcasted_iota(jnp.int32, (rows, cols), 1)
    for copy in fetch[2:10]:
        copy.wait()
    mine = own[...].reshape(rows, width)
    for group in ((0,), (1, 2, 3)):
        for k in group:
            fetch[10 + k].wait()
        for k in group:
            where = slice(k * cols, (k + 1) * cols)
            logits = nt_dot(mine, four[where]) * scale
            col = stat_ref[first + (place ^ k), :, every + LANES :]
            weights[:, where] = weigh(logits, row, col, match - at_ref[1 + k] == ids)
    peak = jnp.max(stat_ref[:, 0, every : every + LANES], axis=0, keepdims=True)
    down_ref[...] = down_scale(peak)
    part = jnp.dot(weights[...], four[...], preferred_element_type=F32) * up_scale(peak[:, :1])
    a_ref[...] = part[: 4 * per].astype(a_ref.dtype).reshape(a_ref.shape)
    b_ref[...] = part[4 * per : 6 * per].reshape(b_ref.shape)
    c_ref[...] = part[6 * per : 7 * per]
    d_ref[...] = part[7 * per :]


def image_call(at, stats, match, images, texts, scale):
    rows, width = images.shape
    cols = texts[0].shape[0]
    own = rows // 4
    per = rows // 32
    outs = [(4, per, width), (2, per, width), (per, width), (per, width), (1, LANES)]
    kinds = [BF16, F32, F32, F32, F32]
    return pl.pallas_call(
        functools.partial(image_kernel, scale),
        in_specs=[SCALARS] + [HBM] * 7,
        out_specs=[VMEM] * 5,
        out_shape=[jax.ShapeDtypeStruct(s, t) for s, t in zip(outs, kinds)],
        scratch_shapes=[
            pltpu.VMEM(stats.shape, F32),
            pltpu.VMEM(match.shape, jnp.int32),
            pltpu.VMEM((8, per, width), BF16),
            pltpu.VMEM((4 * cols, width), BF16),
            pltpu.VMEM((8, per, 1), F32),
            pltpu.VMEM((8, per, 1), jnp.int32),
            pltpu.VMEM((own, 4 * cols), BF16),
            pltpu.SemaphoreType.DMA((7,)),
        ],
        compiler_params=params(60),
        cost_estimate=FREE,
        name="image_part",
    )(at, stats, match, images.reshape(8, 4, per, width), *texts)


def shards(images, texts, match):
    rows, width = images.shape
    cols = texts.shape[0]
    scale = 2.0 / math.sqrt(width) * LOG2E
    zhi, zb, za, yhi, core = (lax.axis_index(a) for a in TXT)
    place = yhi * 2 + core
    z = zhi * 4 + zb * 2 + za

    other_yhi = swap(texts, "yhi")
    other_core = swap(texts, "core")

    logits, row, col = first_call(texts, images, scale)
    cross = z_swap(row, (7, 7))
    row = merge(row, cross, rows)
    near = z_swap(row, (1, 1))
    got = exchange(col, IMG)
    sent = merge_call(got, row, near)
    other_yhi, sent = tie(other_yhi, sent)
    stats = exchange(sent, ("zb", "yhi", "core"))
    other_both = swap(other_yhi, "core")

    bases = [(z * 4 + (place ^ k)) * cols for k in range(4)]
    at = jnp.stack([place, *bases, z, core, zb * 4])
    match = match[None]
    a, b, c, d, down = image_call(at, stats, match, images, (texts, other_core, other_yhi, other_both), scale)
    text_parts = text_call(at, logits, stats, match, images, d)

    a = z_swap(a, (1, 2))
    b = (b + a[2:].astype(F32)).astype(F16)
    b = z_swap(b, (2, 1))
    c = c + a[1].astype(F32)
    d = d + a[0].astype(F32)
    text_parts = exchange(text_parts, IMG)
    b, c, d = tie(b, c, d)
    c = z_swap((c + b[1].astype(F32)).astype(F16), (7, 7))
    d = d + b[0].astype(F32)
    text_grad = jnp.sum(text_parts.astype(F32), axis=0)
    c, d = tie(c, d)
    return (d + c.astype(F32)) * down[:, :1], text_grad


def solution(mesh):
    fine = Mesh(mesh.devices.reshape(SIZES), AXES)
    in_specs = (P(IMG, None), P(TXT, None), P(IMG))
    out_specs = (P(IMG + TXT, None), P(TXT + IMG, None))
    return jax.shard_map(shards, mesh=fine, in_specs=in_specs, out_specs=out_specs, check_vma=False)
```

```python
import functools
import math

import jax
import jax.numpy as jnp
from jax import lax
from jax.experimental import pallas as pl
from jax.experimental.pallas import tpu as pltpu
from jax.sharding import Mesh, PartitionSpec as P

AXES = ("ylo", "x", "zhi", "zb", "za", "yhi", "core")
SIZES = (2, 4, 2, 2, 2, 2, 2)
IMG = ("ylo", "x")
TXT = ("zhi", "zb", "za", "yhi", "core")
F32 = jnp.float32
BF16 = jnp.bfloat16
F16 = jnp.float16
LOG2E = 1.4426950408889634
HBM = pl.BlockSpec(memory_space=pltpu.HBM)
ANY = pl.BlockSpec(memory_space=pl.ANY)
VMEM = pl.BlockSpec(memory_space=pltpu.VMEM)
SCALARS = pl.BlockSpec(memory_space=pltpu.SMEM)
FREE = pl.CostEstimate(flops=0, bytes_accessed=0, transcendentals=0)
LANES = 128
MIB = 1024 * 1024


def swap(value, axis):
    return lax.ppermute(value, axis, [(0, 1), (1, 0)])


def z_swap(value, bits):
    pairs = [(z * 2 + c, (z ^ bits[c]) * 2 + c) for z in range(8) for c in range(2)]
    return lax.ppermute(value, ("zhi", "zb", "za", "core"), pairs)


def exchange(copies, axes):
    return lax.all_to_all(copies, axes, 0, 0, tiled=True)


def tie(*values):
    return lax.optimization_barrier(values)


def log2_sum(values, axis):
    top = jnp.max(values, axis=axis, keepdims=True)
    return top + jnp.log2(jnp.sum(jnp.exp2(values - top), axis=axis, keepdims=True))


def merge(own, got, n):
    top = jnp.maximum(own, got)
    total = top + jnp.log2(jnp.exp2(own - top) + jnp.exp2(got - top))
    lanes = lax.broadcasted_iota(jnp.int32, own.shape, 1)
    return jnp.where(lanes < n, total, top)


def params(mib):
    return pltpu.CompilerParams(vmem_limit_bytes=mib * MIB)


def nt_dot(a, b):
    return lax.dot_general(a, b, (((1,), (1,)), ((), ())), preferred_element_type=F32)


def largest(block):
    peak = jnp.max(jnp.abs(block).astype(F32), axis=0, keepdims=True)
    return jnp.max(peak, axis=1, keepdims=True)


def first_kernel(scale, text_in, image_in, logits_out, row_ref, col_ref, text_ref, image_ref, logits_ref, sems):
    cols = text_in.shape[0]
    rows = image_in.shape[0]
    size = rows // 3
    steps = range(0, rows, size)
    fetch = [pltpu.make_async_copy(text_in, text_ref, sems.at[0])]
    fetch += [
        pltpu.make_async_copy(image_in.at[pl.ds(j, size)], image_ref.at[pl.ds(j, size)], sems.at[1 + k])
        for k, j in enumerate(steps)
    ]
    for copy in fetch:
        copy.start()
    fetch[0].wait()
    text = text_ref[...]
    row_ref[:, rows:] = jnp.broadcast_to(largest(text), (1, LANES))
    high = total = None
    store = []
    for k in range(len(steps) + 1):
        if k < len(steps):
            fetch[1 + k].wait()
            where = pl.ds(steps[k], size)
            logits_ref[:, where] = nt_dot(text, image_ref[where]) * scale
            store.append(pltpu.make_async_copy(logits_ref.at[:, where], logits_out.at[:, where], sems.at[4 + k]))
            store[k].start()
        if k == 0:
            continue
        j = steps[k - 1]
        logits = logits_ref[:, j : j + size]
        deep = logits.reshape(cols // 8, 8, size)
        top = jnp.max(deep, axis=0)
        part = jnp.sum(jnp.exp2(deep - top[None]), axis=0)
        best = jnp.max(top, axis=0, keepdims=True)
        part = jnp.sum(part * jnp.exp2(top - best), axis=0, keepdims=True)
        row_ref[:, j : j + size] = best + jnp.log2(part)
        tiles = [logits[:, i : i + LANES] for i in range(0, size, LANES)]
        new = functools.reduce(jnp.maximum, tiles if high is None else [high, *tiles])
        sums = [jnp.exp2(tile - new) for tile in tiles]
        total = functools.reduce(jnp.add, sums if high is None else [total * jnp.exp2(high - new), *sums])
        high = new
    best = jnp.max(high, axis=1, keepdims=True)
    share = best + jnp.log2(jnp.sum(total * jnp.exp2(high - best), axis=1, keepdims=True))
    share = jnp.transpose(jnp.broadcast_to(share, (cols, LANES)))[:1]
    for k in range(col_ref.shape[0]):
        col_ref[k] = share
    for copy in store:
        copy.wait()


def first_call(texts, images, scale):
    cols = texts.shape[0]
    rows = images.shape[0]
    outs = [(cols, rows), (1, rows + LANES), (8, 1, cols)]
    return pl.pallas_call(
        functools.partial(first_kernel, scale),
        in_specs=[HBM] * 2,
        out_specs=[HBM, VMEM, VMEM],
        out_shape=[jax.ShapeDtypeStruct(s, F32) for s in outs],
        scratch_shapes=[
            pltpu.VMEM(texts.shape, BF16),
            pltpu.VMEM(images.shape, BF16),
            pltpu.VMEM((cols, rows), F32),
            pltpu.SemaphoreType.DMA((7,)),
        ],
        compiler_params=params(60),
        cost_estimate=FREE,
        name="logits",
    )(texts, images)


def merge_kernel(got_ref, row_ref, near_ref, out_ref):
    rows = row_ref.shape[1]
    col = log2_sum(got_ref[:, 0, :], 0)
    both = merge(row_ref[...], near_ref[...], rows - LANES)
    for k in range(out_ref.shape[0]):
        out_ref[k, :, :rows] = both
        out_ref[k, :, rows:] = col


def merge_call(got, row, near):
    cols = got.shape[2]
    return pl.pallas_call(
        merge_kernel,
        in_specs=[VMEM] * 3,
        out_specs=VMEM,
        out_shape=jax.ShapeDtypeStruct((8, 1, row.shape[1] + cols), F32),
        compiler_params=params(4),
        cost_estimate=FREE,
        name="merge",
    )(got, row, near)


def weigh(logits, row, col, paired):
    total = jnp.exp2(logits - row) + jnp.exp2(logits - col)
    return (0.5 * total - paired.astype(F32)).astype(BF16)


def up_scale(peak):
    return 8.0 / jnp.maximum(peak, 1e-30)


def down_scale(peak):
    return jnp.maximum(peak, 1e-30) * 0.125


def text_kernel(at_ref, logits_in, stat_in, match_in, image_in, after_ref, out_ref, stat_ref, match_ref, logits_ref, image_ref, weights, sems):
    cols, rows = logits_in.shape
    size = rows // 4
    steps = range(0, rows, size)
    fetch = [
        pltpu.make_async_copy(logits_in.at[:, pl.ds(j, size)], logits_ref.at[:, pl.ds(j, size)], sems.at[k])
        for k, j in enumerate(steps)
    ]
    fetch.append(pltpu.make_async_copy(image_in, image_ref, sems.at[4]))
    facts = [pltpu.make_async_copy(stat_in, stat_ref, sems.at[5]), pltpu.make_async_copy(match_in, match_ref, sems.at[6])]
    for copy in facts + fetch:
        copy.start()
    for copy in facts:
        copy.wait()
    row = log2_sum(stat_ref[:, 0, :rows], 0)
    col = stat_ref[at_ref[7] + at_ref[0], :, rows + LANES :]
    col = jnp.transpose(jnp.broadcast_to(col, (LANES, cols)))[:, :1]
    ids = at_ref[1] + lax.broadcasted_iota(jnp.int32, (cols, size), 0)
    for k, j in enumerate(steps):
        fetch[k].wait()
        paired = match_ref[:, j : j + size] == ids
        weights[:, j : j + size] = weigh(logits_ref[:, j : j + size], row[:, j : j + size], col, paired)
    fetch[4].wait()
    part = jnp.dot(weights[...], image_ref[...], preferred_element_type=F32)
    out_ref[...] = part.astype(BF16).reshape(out_ref.shape)


def text_call(at, logits, stats, match, images, after):
    cols, rows = logits.shape
    width = images.shape[1]
    return pl.pallas_call(
        text_kernel,
        in_specs=[SCALARS, HBM, ANY, ANY, HBM, ANY],
        out_specs=VMEM,
        out_shape=jax.ShapeDtypeStruct((8, cols // 8, width), BF16),
        scratch_shapes=[
            pltpu.VMEM(stats.shape, F32),
            pltpu.VMEM(match.shape, jnp.int32),
            pltpu.VMEM((cols, rows), F32),
            pltpu.VMEM(images.shape, BF16),
            pltpu.VMEM((cols, rows), BF16),
            pltpu.SemaphoreType.DMA((7,)),
        ],
        compiler_params=params(50),
        cost_estimate=FREE,
        name="text_part",
    )(at, logits, stats, match, images, after)


def image_kernel(scale, at_ref, stat_in, match_in, image_ref, t0, t1, t2, t3, a_ref, b_ref, c_ref, d_ref, down_ref, stat_ref, match_ref, own, four, row_by, match_by, weights, sems):
    texts = (t0, t1, t2, t3)
    blocks, _, per, width = image_ref.shape
    cols = t0.shape[0]
    rows = blocks * per
    every = match_in.shape[1]
    place, z, core, first = at_ref[0], at_ref[5], at_ref[6], at_ref[7]
    one, two = 1 + core, 2 - core
    order = [z ^ one, z ^ one ^ 7, z ^ 3, z ^ 4, z ^ two, z ^ two ^ 7, z ^ 7, z]
    fetch = [
        pltpu.make_async_copy(stat_in, stat_ref, sems.at[5]),
        pltpu.make_async_copy(match_in, match_ref, sems.at[6]),
    ]
    fetch += [
        pltpu.make_async_copy(image_ref.at[block, place], own.at[k], sems.at[4]) for k, block in enumerate(order)
    ]
    fetch += [
        pltpu.make_async_copy(texts[k], four.at[pl.ds(k * cols, cols)], sems.at[k]) for k in range(4)
    ]
    for copy in fetch:
        copy.start()
    fetch[0].wait()
    fetch[1].wait()
    row_all = log2_sum(stat_ref[:, 0, :every], 0)
    pair = lax.broadcasted_iota(jnp.int32, (2 * per, 1), 0)
    lane = pair + jnp.where(pair < per, 0, 3 * per) + place * per
    wanted = lax.broadcasted_iota(jnp.int32, (2 * per, 8 * per), 1) == lane
    for k, j in enumerate(range(0, every, 8 * per)):
        window = slice(j, j + 8 * per)
        row = jnp.sum(jnp.where(wanted, row_all[:, window], 0.0), axis=1, keepdims=True)
        match = jnp.sum(jnp.where(wanted, match_ref[:, window], 0), axis=1, keepdims=True)
        row_by[2 * k : 2 * k + 2] = row.reshape(2, per, 1)
        match_by[2 * k : 2 * k + 2] = match.reshape(2, per, 1)
    row = jnp.concatenate([row_by[block] for block in order], axis=0)
    match = jnp.concatenate([match_by[block] for block in order], axis=0)
    ids = lax.broadcasted_iota(jnp.int32, (rows, cols), 1)
    for copy in fetch[2:10]:
        copy.wait()
    mine = own[...].reshape(rows, width)
    for group in ((0,), (1, 2, 3)):
        for k in group:
            fetch[10 + k].wait()
        for k in group:
            where = slice(k * cols, (k + 1) * cols)
            logits = nt_dot(mine, four[where]) * scale
            col = stat_ref[first + (place ^ k), :, every + LANES :]
            weights[:, where] = weigh(logits, row, col, match - at_ref[1 + k] == ids)
    peak = jnp.max(stat_ref[:, 0, every : every + LANES], axis=0, keepdims=True)
    down_ref[...] = down_scale(peak)
    part = jnp.dot(weights[...], four[...], preferred_element_type=F32) * up_scale(peak[:, :1])
    a_ref[...] = part[: 4 * per].astype(a_ref.dtype).reshape(a_ref.shape)
    b_ref[...] = part[4 * per : 6 * per].reshape(b_ref.shape)
    c_ref[...] = part[6 * per : 7 * per]
    d_ref[...] = part[7 * per :]


def image_call(at, stats, match, images, texts, scale):
    rows, width = images.shape
    cols = texts[0].shape[0]
    own = rows // 4
    per = rows // 32
    outs = [(4, per, width), (2, per, width), (per, width), (per, width), (1, LANES)]
    kinds = [BF16, F32, F32, F32, F32]
    return pl.pallas_call(
        functools.partial(image_kernel, scale),
        in_specs=[SCALARS, ANY, ANY] + [HBM] * 5,
        out_specs=[VMEM] * 5,
        out_shape=[jax.ShapeDtypeStruct(s, t) for s, t in zip(outs, kinds)],
        scratch_shapes=[
            pltpu.VMEM(stats.shape, F32),
            pltpu.VMEM(match.shape, jnp.int32),
            pltpu.VMEM((8, per, width), BF16),
            pltpu.VMEM((4 * cols, width), BF16),
            pltpu.VMEM((8, per, 1), F32),
            pltpu.VMEM((8, per, 1), jnp.int32),
            pltpu.VMEM((own, 4 * cols), BF16),
            pltpu.SemaphoreType.DMA((7,)),
        ],
        compiler_params=params(50),
        cost_estimate=FREE,
        name="image_part",
    )(at, stats, match, images.reshape(8, 4, per, width), *texts)


def shards(images, texts, match):
    rows, width = images.shape
    cols = texts.shape[0]
    scale = 2.0 / math.sqrt(width) * LOG2E
    zhi, zb, za, yhi, core = (lax.axis_index(a) for a in TXT)
    place = yhi * 2 + core
    z = zhi * 4 + zb * 2 + za

    other_yhi = swap(texts, "yhi")
    other_core = swap(texts, "core")

    logits, row, col = first_call(texts, images, scale)
    cross = z_swap(row, (7, 7))
    row = merge(row, cross, rows)
    near = z_swap(row, (1, 1))
    got = exchange(col, IMG)
    sent = merge_call(got, row, near)
    other_yhi, sent = tie(other_yhi, sent)
    stats = exchange(sent, ("zb", "yhi", "core"))
    other_both = swap(other_yhi, "core")

    bases = [(z * 4 + (place ^ k)) * cols for k in range(4)]
    at = jnp.stack([place, *bases, z, core, zb * 4])
    match = match[None]
    a, b, c, d, down = image_call(at, stats, match, images, (texts, other_core, other_yhi, other_both), scale)
    text_parts = text_call(at, logits, stats, match, images, down)

    a = z_swap(a, (1, 2))
    b = (b + a[2:].astype(F32)).astype(F16)
    b = z_swap(b, (2, 1))
    c = c + a[1].astype(F32)
    d = d + a[0].astype(F32)
    text_parts = exchange(text_parts, IMG)
    b, c, d = tie(b, c, d)
    c = z_swap((c + b[1].astype(F32)).astype(F16), (7, 7))
    d = d + b[0].astype(F32)
    text_grad = jnp.sum(text_parts.astype(F32), axis=0)
    c, d = tie(c, d)
    return (d + c.astype(F32)) * down[:, :1], text_grad


def solution(mesh):
    fine = Mesh(mesh.devices.reshape(SIZES), AXES)
    in_specs = (P(IMG, None), P(TXT, None), P(IMG))
    out_specs = (P(IMG + TXT, None), P(TXT + IMG, None))
    return jax.shard_map(shards, mesh=fine, in_specs=in_specs, out_specs=out_specs, check_vma=False)
```

```python
import functools
import math

import jax
import jax.numpy as jnp
from jax import lax
from jax.experimental import pallas as pl
from jax.experimental.pallas import tpu as pltpu
from jax.sharding import Mesh, PartitionSpec as P

AXES = ("ylo", "x", "zhi", "zb", "za", "yhi", "core")
SIZES = (2, 4, 2, 2, 2, 2, 2)
IMG = ("ylo", "x")
TXT = ("zhi", "zb", "za", "yhi", "core")
F32 = jnp.float32
BF16 = jnp.bfloat16
F16 = jnp.float16
LOG2E = 1.4426950408889634
HBM = pl.BlockSpec(memory_space=pltpu.HBM)
ANY = pl.BlockSpec(memory_space=pl.ANY)
VMEM = pl.BlockSpec(memory_space=pltpu.VMEM)
SCALARS = pl.BlockSpec(memory_space=pltpu.SMEM)
FREE = pl.CostEstimate(flops=0, bytes_accessed=0, transcendentals=0)
LANES = 128
MIB = 1024 * 1024


def swap(value, axis):
    return lax.ppermute(value, axis, [(0, 1), (1, 0)])


def z_swap(value, bits):
    pairs = [(z * 2 + c, (z ^ bits[c]) * 2 + c) for z in range(8) for c in range(2)]
    return lax.ppermute(value, ("zhi", "zb", "za", "core"), pairs)


def exchange(copies, axes):
    return lax.all_to_all(copies, axes, 0, 0, tiled=True)


def tie(*values):
    return lax.optimization_barrier(values)


def log2_sum(values, axis):
    top = jnp.max(values, axis=axis, keepdims=True)
    return top + jnp.log2(jnp.sum(jnp.exp2(values - top), axis=axis, keepdims=True))


def merge(own, got, n):
    top = jnp.maximum(own, got)
    total = top + jnp.log2(jnp.exp2(own - top) + jnp.exp2(got - top))
    lanes = lax.broadcasted_iota(jnp.int32, own.shape, 1)
    return jnp.where(lanes < n, total, top)


def params(mib):
    return pltpu.CompilerParams(vmem_limit_bytes=mib * MIB)


def nt_dot(a, b):
    return lax.dot_general(a, b, (((1,), (1,)), ((), ())), preferred_element_type=F32)


def largest(block):
    peak = jnp.max(jnp.abs(block).astype(F32), axis=0, keepdims=True)
    return jnp.max(peak, axis=1, keepdims=True)


def first_kernel(scale, text_in, image_in, logits_out, row_ref, col_ref, text_ref, image_ref, logits_ref, sems):
    cols = text_in.shape[0]
    rows = image_in.shape[0]
    size = rows // 3
    steps = range(0, rows, size)
    fetch = [pltpu.make_async_copy(text_in, text_ref, sems.at[0])]
    fetch += [
        pltpu.make_async_copy(image_in.at[pl.ds(j, size)], image_ref.at[pl.ds(j, size)], sems.at[1 + k])
        for k, j in enumerate(steps)
    ]
    for copy in fetch:
        copy.start()
    fetch[0].wait()
    text = text_ref[...]
    row_ref[:, rows:] = jnp.broadcast_to(largest(text), (1, LANES))
    high = total = None
    store = []
    for k in range(len(steps) + 1):
        if k < len(steps):
            fetch[1 + k].wait()
            where = pl.ds(steps[k], size)
            logits_ref[:, where] = nt_dot(text, image_ref[where]) * scale
            store.append(pltpu.make_async_copy(logits_ref.at[:, where], logits_out.at[:, where], sems.at[4 + k]))
            store[k].start()
        if k == 0:
            continue
        j = steps[k - 1]
        logits = logits_ref[:, j : j + size]
        deep = logits.reshape(cols // 8, 8, size)
        top = jnp.max(deep, axis=0)
        part = jnp.sum(jnp.exp2(deep - top[None]), axis=0)
        best = jnp.max(top, axis=0, keepdims=True)
        part = jnp.sum(part * jnp.exp2(top - best), axis=0, keepdims=True)
        row_ref[:, j : j + size] = best + jnp.log2(part)
        tiles = [logits[:, i : i + LANES] for i in range(0, size, LANES)]
        new = functools.reduce(jnp.maximum, tiles if high is None else [high, *tiles])
        sums = [jnp.exp2(tile - new) for tile in tiles]
        total = functools.reduce(jnp.add, sums if high is None else [total * jnp.exp2(high - new), *sums])
        high = new
    best = jnp.max(high, axis=1, keepdims=True)
    share = best + jnp.log2(jnp.sum(total * jnp.exp2(high - best), axis=1, keepdims=True))
    share = jnp.transpose(jnp.broadcast_to(share, (cols, LANES)))[:1]
    for k in range(col_ref.shape[0]):
        col_ref[k] = share
    for copy in store:
        copy.wait()


def first_call(texts, images, scale):
    cols = texts.shape[0]
    rows = images.shape[0]
    outs = [(cols, rows), (1, rows + LANES), (8, 1, cols)]
    return pl.pallas_call(
        functools.partial(first_kernel, scale),
        in_specs=[HBM] * 2,
        out_specs=[HBM, VMEM, VMEM],
        out_shape=[jax.ShapeDtypeStruct(s, F32) for s in outs],
        scratch_shapes=[
            pltpu.VMEM(texts.shape, BF16),
            pltpu.VMEM(images.shape, BF16),
            pltpu.VMEM((cols, rows), F32),
            pltpu.SemaphoreType.DMA((7,)),
        ],
        compiler_params=params(60),
        cost_estimate=FREE,
        name="logits",
    )(texts, images)


def merge_kernel(got_ref, row_ref, near_ref, out_ref):
    rows = row_ref.shape[1]
    col = log2_sum(got_ref[:, 0, :], 0)
    both = merge(row_ref[...], near_ref[...], rows - LANES)
    for k in range(out_ref.shape[0]):
        out_ref[k, :, :rows] = both
        out_ref[k, :, rows:] = col


def merge_call(got, row, near):
    cols = got.shape[2]
    return pl.pallas_call(
        merge_kernel,
        in_specs=[VMEM] * 3,
        out_specs=VMEM,
        out_shape=jax.ShapeDtypeStruct((8, 1, row.shape[1] + cols), F32),
        compiler_params=params(4),
        cost_estimate=FREE,
        name="merge",
    )(got, row, near)


def weigh(logits, row, col, paired):
    total = jnp.exp2(logits - row) + jnp.exp2(logits - col)
    return (0.5 * total - paired.astype(F32)).astype(BF16)


def up_scale(peak):
    return 8.0 / jnp.maximum(peak, 1e-30)


def down_scale(peak):
    return jnp.maximum(peak, 1e-30) * 0.125


def text_kernel(at_ref, logits_in, stat_in, match_in, image_in, after_ref, out_ref, stat_ref, match_ref, logits_ref, image_ref, weights, sems):
    cols, rows = logits_in.shape
    size = rows // 4
    steps = range(0, rows, size)
    fetch = [
        pltpu.make_async_copy(logits_in.at[:, pl.ds(j, size)], logits_ref.at[:, pl.ds(j, size)], sems.at[k])
        for k, j in enumerate(steps)
    ]
    fetch.append(pltpu.make_async_copy(image_in, image_ref, sems.at[4]))
    facts = [pltpu.make_async_copy(stat_in, stat_ref, sems.at[5]), pltpu.make_async_copy(match_in, match_ref, sems.at[6])]
    for copy in facts + fetch:
        copy.start()
    for copy in facts:
        copy.wait()
    row = log2_sum(stat_ref[:, 0, :rows], 0)
    col = stat_ref[at_ref[7] + at_ref[0], :, rows + LANES :]
    col = jnp.transpose(jnp.broadcast_to(col, (LANES, cols)))[:, :1]
    ids = at_ref[1] + lax.broadcasted_iota(jnp.int32, (cols, size), 0)
    for k, j in enumerate(steps):
        fetch[k].wait()
        paired = match_ref[:, j : j + size] == ids
        weights[:, j : j + size] = weigh(logits_ref[:, j : j + size], row[:, j : j + size], col, paired)
    fetch[4].wait()
    part = jnp.dot(weights[...], image_ref[...], preferred_element_type=F32)
    out_ref[...] = part.astype(BF16).reshape(out_ref.shape)


def text_call(at, logits, stats, match, images, after):
    cols, rows = logits.shape
    width = images.shape[1]
    return pl.pallas_call(
        text_kernel,
        in_specs=[SCALARS, HBM, ANY, ANY, HBM, ANY],
        out_specs=VMEM,
        out_shape=jax.ShapeDtypeStruct((8, cols // 8, width), BF16),
        scratch_shapes=[
            pltpu.VMEM(stats.shape, F32),
            pltpu.VMEM(match.shape, jnp.int32),
            pltpu.VMEM((cols, rows), F32),
            pltpu.VMEM(images.shape, BF16),
            pltpu.VMEM((cols, rows), BF16),
            pltpu.SemaphoreType.DMA((7,)),
        ],
        compiler_params=params(50),
        cost_estimate=FREE,
        name="text_part",
    )(at, logits, stats, match, images, after)


def settle_kernel(in_ref, out_ref, sem):
    copy = pltpu.make_async_copy(in_ref, out_ref, sem)
    copy.start()
    copy.wait()


def settle(value):
    return pl.pallas_call(
        settle_kernel,
        in_specs=[VMEM],
        out_specs=HBM,
        out_shape=jax.ShapeDtypeStruct(value.shape, value.dtype),
        scratch_shapes=[pltpu.SemaphoreType.DMA],
        cost_estimate=FREE,
        name="settle",
    )(value)


def image_kernel(scale, at_ref, stat_in, match_in, image_ref, t0, t1, t2, t3, e_ref, a_ref, b_ref, c_ref, d_ref, down_ref, stat_ref, match_ref, own, four, row_by, match_by, weights, sems):
    texts = (t0, t1, t2, t3)
    blocks, _, per, width = image_ref.shape
    cols = t0.shape[0]
    rows = blocks * per
    every = match_in.shape[1]
    place, z, core, first = at_ref[0], at_ref[5], at_ref[6], at_ref[7]
    one, two = 1 + core, 2 - core
    order = [z ^ 3, z ^ 4, z ^ one, z ^ one ^ 7, z ^ two, z ^ two ^ 7, z ^ 7, z]
    fetch = [
        pltpu.make_async_copy(stat_in, stat_ref, sems.at[5]),
        pltpu.make_async_copy(match_in, match_ref, sems.at[6]),
    ]
    fetch += [
        pltpu.make_async_copy(image_ref.at[block, place], own.at[k], sems.at[4]) for k, block in enumerate(order)
    ]
    fetch += [
        pltpu.make_async_copy(texts[k], four.at[pl.ds(k * cols, cols)], sems.at[k]) for k in range(4)
    ]
    for copy in fetch:
        copy.start()
    fetch[0].wait()
    fetch[1].wait()
    row_all = log2_sum(stat_ref[:, 0, :every], 0)
    pair = lax.broadcasted_iota(jnp.int32, (2 * per, 1), 0)
    lane = pair + jnp.where(pair < per, 0, 3 * per) + place * per
    wanted = lax.broadcasted_iota(jnp.int32, (2 * per, 8 * per), 1) == lane
    for k, j in enumerate(range(0, every, 8 * per)):
        window = slice(j, j + 8 * per)
        row = jnp.sum(jnp.where(wanted, row_all[:, window], 0.0), axis=1, keepdims=True)
        match = jnp.sum(jnp.where(wanted, match_ref[:, window], 0), axis=1, keepdims=True)
        row_by[2 * k : 2 * k + 2] = row.reshape(2, per, 1)
        match_by[2 * k : 2 * k + 2] = match.reshape(2, per, 1)
    row = jnp.concatenate([row_by[block] for block in order], axis=0)
    match = jnp.concatenate([match_by[block] for block in order], axis=0)
    ids = lax.broadcasted_iota(jnp.int32, (rows, cols), 1)
    for copy in fetch[2:10]:
        copy.wait()
    mine = own[...].reshape(rows, width)
    for group in ((0,), (1, 2, 3)):
        for k in group:
            fetch[10 + k].wait()
        for k in group:
            where = slice(k * cols, (k + 1) * cols)
            logits = nt_dot(mine, four[where]) * scale
            col = stat_ref[first + (place ^ k), :, every + LANES :]
            weights[:, where] = weigh(logits, row, col, match - at_ref[1 + k] == ids)
    peak = jnp.max(stat_ref[:, 0, every : every + LANES], axis=0, keepdims=True)
    down_ref[...] = down_scale(peak)
    part = jnp.dot(weights[...], four[...], preferred_element_type=F32) * up_scale(peak[:, :1])
    e_ref[...] = part[: 2 * per].astype(e_ref.dtype).reshape(e_ref.shape)
    a_ref[...] = part[2 * per : 4 * per].astype(a_ref.dtype).reshape(a_ref.shape)
    b_ref[...] = part[4 * per : 6 * per].reshape(b_ref.shape)
    c_ref[...] = part[6 * per : 7 * per]
    d_ref[...] = part[7 * per :]


def image_call(at, stats, match, images, texts, scale):
    rows, width = images.shape
    cols = texts[0].shape[0]
    own = rows // 4
    per = rows // 32
    outs = [(2, per, width), (2, per, width), (2, per, width), (per, width), (per, width), (1, LANES)]
    kinds = [BF16, BF16, F32, F32, F32, F32]
    return pl.pallas_call(
        functools.partial(image_kernel, scale),
        in_specs=[SCALARS, ANY, ANY] + [HBM] * 5,
        out_specs=[VMEM] * 6,
        out_shape=[jax.ShapeDtypeStruct(s, t) for s, t in zip(outs, kinds)],
        scratch_shapes=[
            pltpu.VMEM(stats.shape, F32),
            pltpu.VMEM(match.shape, jnp.int32),
            pltpu.VMEM((8, per, width), BF16),
            pltpu.VMEM((4 * cols, width), BF16),
            pltpu.VMEM((8, per, 1), F32),
            pltpu.VMEM((8, per, 1), jnp.int32),
            pltpu.VMEM((own, 4 * cols), BF16),
            pltpu.SemaphoreType.DMA((7,)),
        ],
        compiler_params=params(50),
        cost_estimate=FREE,
        name="image_part",
    )(at, stats, match, images.reshape(8, 4, per, width), *texts)


def shards(images, texts, match):
    rows, width = images.shape
    cols = texts.shape[0]
    scale = 2.0 / math.sqrt(width) * LOG2E
    zhi, zb, za, yhi, core = (lax.axis_index(a) for a in TXT)
    place = yhi * 2 + core
    z = zhi * 4 + zb * 2 + za

    other_yhi = swap(texts, "yhi")
    other_core = swap(texts, "core")

    logits, row, col = first_call(texts, images, scale)
    cross = z_swap(row, (7, 7))
    row = merge(row, cross, rows)
    near = z_swap(row, (1, 1))
    got = exchange(col, IMG)
    sent = merge_call(got, row, near)
    other_yhi, sent = tie(other_yhi, sent)
    stats = exchange(sent, ("zb", "yhi", "core"))
    other_both = settle(swap(other_yhi, "core"))

    bases = [(z * 4 + (place ^ k)) * cols for k in range(4)]
    at = jnp.stack([place, *bases, z, core, zb * 4])
    match = match[None]
    e, a, b, c, d, down = image_call(at, stats, match, images, (texts, other_core, other_yhi, other_both), scale)
    text_parts = text_call(at, logits, stats, match, images, down)

    e = z_swap(e, (1, 2))
    a = z_swap(a, (1, 2))
    e, text_parts = tie(e, text_parts)
    b = (b + e.astype(F32)).astype(F16)
    b, down = tie(b, down)
    b = z_swap(b, (2, 1))
    down = swap(down, "core")
    down, text_parts = tie(down, text_parts)
    c = c + a[1].astype(F32)
    d = d + a[0].astype(F32)
    text_parts = exchange(text_parts, IMG)
    b, c, d = tie(b, c, d)
    c = z_swap((c + b[1].astype(F32)).astype(F16), (7, 7))
    d = d + b[0].astype(F32)
    text_grad = jnp.sum(text_parts.astype(F32), axis=0)
    c, d = tie(c, d)
    return (d + c.astype(F32)) * down[:, :1], text_grad


def solution(mesh):
    fine = Mesh(mesh.devices.reshape(SIZES), AXES)
    in_specs = (P(IMG, None), P(TXT, None), P(IMG))
    out_specs = (P(IMG + TXT, None), P(TXT + IMG, None))
    return jax.shard_map(shards, mesh=fine, in_specs=in_specs, out_specs=out_specs, check_vma=False)
```

```python
import functools
import math

import jax
import jax.numpy as jnp
from jax import lax
from jax.experimental import pallas as pl
from jax.experimental.pallas import tpu as pltpu
from jax.sharding import Mesh, PartitionSpec as P

AXES = ("ylo", "x", "zhi", "zb", "za", "yhi", "core")
SIZES = (2, 4, 2, 2, 2, 2, 2)
IMG = ("ylo", "x")
TXT = ("zhi", "zb", "za", "yhi", "core")
F32 = jnp.float32
BF16 = jnp.bfloat16
F16 = jnp.float16
LOG2E = 1.4426950408889634
HBM = pl.BlockSpec(memory_space=pltpu.HBM)
ANY = pl.BlockSpec(memory_space=pl.ANY)
VMEM = pl.BlockSpec(memory_space=pltpu.VMEM)
SCALARS = pl.BlockSpec(memory_space=pltpu.SMEM)
FREE = pl.CostEstimate(flops=0, bytes_accessed=0, transcendentals=0)
LANES = 128
MIB = 1024 * 1024


def swap(value, axis):
    return lax.ppermute(value, axis, [(0, 1), (1, 0)])


def z_swap(value, bits):
    pairs = [(z * 2 + c, (z ^ bits[c]) * 2 + c) for z in range(8) for c in range(2)]
    return lax.ppermute(value, ("zhi", "zb", "za", "core"), pairs)


def exchange(copies, axes):
    return lax.all_to_all(copies, axes, 0, 0, tiled=True)


def tie(*values):
    return lax.optimization_barrier(values)


def log2_sum(values, axis):
    top = jnp.max(values, axis=axis, keepdims=True)
    return top + jnp.log2(jnp.sum(jnp.exp2(values - top), axis=axis, keepdims=True))


def merge(own, got, n):
    top = jnp.maximum(own, got)
    total = top + jnp.log2(jnp.exp2(own - top) + jnp.exp2(got - top))
    lanes = lax.broadcasted_iota(jnp.int32, own.shape, 1)
    return jnp.where(lanes < n, total, top)


def params(mib):
    return pltpu.CompilerParams(vmem_limit_bytes=mib * MIB)


def nt_dot(a, b):
    return lax.dot_general(a, b, (((1,), (1,)), ((), ())), preferred_element_type=F32)


def largest(block):
    peak = jnp.max(jnp.abs(block).astype(F32), axis=0, keepdims=True)
    return jnp.max(peak, axis=1, keepdims=True)


def first_kernel(scale, text_in, image_in, logits_out, row_ref, col_ref, text_ref, image_ref, logits_ref, sems):
    cols = text_in.shape[0]
    rows = image_in.shape[0]
    size = rows // 3
    steps = range(0, rows, size)
    fetch = [pltpu.make_async_copy(text_in, text_ref, sems.at[0])]
    fetch += [
        pltpu.make_async_copy(image_in.at[pl.ds(j, size)], image_ref.at[pl.ds(j, size)], sems.at[1 + k])
        for k, j in enumerate(steps)
    ]
    for copy in fetch:
        copy.start()
    fetch[0].wait()
    text = text_ref[...]
    row_ref[:, rows:] = jnp.broadcast_to(largest(text), (1, LANES))
    high = total = None
    store = []
    for k in range(len(steps) + 1):
        if k < len(steps):
            fetch[1 + k].wait()
            where = pl.ds(steps[k], size)
            logits_ref[:, where] = nt_dot(text, image_ref[where]) * scale
            store.append(pltpu.make_async_copy(logits_ref.at[:, where], logits_out.at[:, where], sems.at[4 + k]))
            store[k].start()
        if k == 0:
            continue
        j = steps[k - 1]
        logits = logits_ref[:, j : j + size]
        deep = logits.reshape(cols // 8, 8, size)
        top = jnp.max(deep, axis=0)
        part = jnp.sum(jnp.exp2(deep - top[None]), axis=0)
        best = jnp.max(top, axis=0, keepdims=True)
        part = jnp.sum(part * jnp.exp2(top - best), axis=0, keepdims=True)
        row_ref[:, j : j + size] = best + jnp.log2(part)
        tiles = [logits[:, i : i + LANES] for i in range(0, size, LANES)]
        new = functools.reduce(jnp.maximum, tiles if high is None else [high, *tiles])
        sums = [jnp.exp2(tile - new) for tile in tiles]
        total = functools.reduce(jnp.add, sums if high is None else [total * jnp.exp2(high - new), *sums])
        high = new
    best = jnp.max(high, axis=1, keepdims=True)
    share = best + jnp.log2(jnp.sum(total * jnp.exp2(high - best), axis=1, keepdims=True))
    share = jnp.transpose(jnp.broadcast_to(share, (cols, LANES)))[:1]
    for k in range(col_ref.shape[0]):
        col_ref[k] = share
    for copy in store:
        copy.wait()


def first_call(texts, images, scale):
    cols = texts.shape[0]
    rows = images.shape[0]
    outs = [(cols, rows), (1, rows + LANES), (8, 1, cols)]
    return pl.pallas_call(
        functools.partial(first_kernel, scale),
        in_specs=[HBM] * 2,
        out_specs=[HBM, VMEM, VMEM],
        out_shape=[jax.ShapeDtypeStruct(s, F32) for s in outs],
        scratch_shapes=[
            pltpu.VMEM(texts.shape, BF16),
            pltpu.VMEM(images.shape, BF16),
            pltpu.VMEM((cols, rows), F32),
            pltpu.SemaphoreType.DMA((7,)),
        ],
        compiler_params=params(60),
        cost_estimate=FREE,
        name="logits",
    )(texts, images)


def merge_kernel(got_ref, row_ref, near_ref, out_ref):
    rows = row_ref.shape[1]
    col = log2_sum(got_ref[:, 0, :], 0)
    both = merge(row_ref[...], near_ref[...], rows - LANES)
    for k in range(out_ref.shape[0]):
        out_ref[k, :, :rows] = both
        out_ref[k, :, rows:] = col


def merge_call(got, row, near):
    cols = got.shape[2]
    return pl.pallas_call(
        merge_kernel,
        in_specs=[VMEM] * 3,
        out_specs=VMEM,
        out_shape=jax.ShapeDtypeStruct((8, 1, row.shape[1] + cols), F32),
        compiler_params=params(4),
        cost_estimate=FREE,
        name="merge",
    )(got, row, near)


def weigh(logits, row, col, paired):
    total = jnp.exp2(logits - row) + jnp.exp2(logits - col)
    return (0.5 * total - paired.astype(F32)).astype(BF16)


def up_scale(peak):
    return 8.0 / jnp.maximum(peak, 1e-30)


def down_scale(peak):
    return jnp.maximum(peak, 1e-30) * 0.125


def text_kernel(at_ref, logits_in, stat_in, match_in, image_in, after_ref, out_ref, stat_ref, match_ref, logits_ref, image_ref, weights, sems):
    cols, rows = logits_in.shape
    size = rows // 4
    steps = range(0, rows, size)
    fetch = [
        pltpu.make_async_copy(logits_in.at[:, pl.ds(j, size)], logits_ref.at[:, pl.ds(j, size)], sems.at[k])
        for k, j in enumerate(steps)
    ]
    fetch.append(pltpu.make_async_copy(image_in, image_ref, sems.at[4]))
    facts = [pltpu.make_async_copy(stat_in, stat_ref, sems.at[5]), pltpu.make_async_copy(match_in, match_ref, sems.at[6])]
    for copy in facts + fetch:
        copy.start()
    for copy in facts:
        copy.wait()
    row = log2_sum(stat_ref[:, 0, :rows], 0)
    col = stat_ref[at_ref[7] + at_ref[0], :, rows + LANES :]
    col = jnp.transpose(jnp.broadcast_to(col, (LANES, cols)))[:, :1]
    ids = at_ref[1] + lax.broadcasted_iota(jnp.int32, (cols, size), 0)
    for k, j in enumerate(steps):
        fetch[k].wait()
        paired = match_ref[:, j : j + size] == ids
        weights[:, j : j + size] = weigh(logits_ref[:, j : j + size], row[:, j : j + size], col, paired)
    fetch[4].wait()
    part = jnp.dot(weights[...], image_ref[...], preferred_element_type=F32)
    out_ref[...] = part.astype(BF16).reshape(out_ref.shape)


def text_call(at, logits, stats, match, images, after):
    cols, rows = logits.shape
    width = images.shape[1]
    return pl.pallas_call(
        text_kernel,
        in_specs=[SCALARS, HBM, ANY, ANY, HBM, ANY],
        out_specs=VMEM,
        out_shape=jax.ShapeDtypeStruct((8, cols // 8, width), BF16),
        scratch_shapes=[
            pltpu.VMEM(stats.shape, F32),
            pltpu.VMEM(match.shape, jnp.int32),
            pltpu.VMEM((cols, rows), F32),
            pltpu.VMEM(images.shape, BF16),
            pltpu.VMEM((cols, rows), BF16),
            pltpu.SemaphoreType.DMA((7,)),
        ],
        compiler_params=params(50),
        cost_estimate=FREE,
        name="text_part",
    )(at, logits, stats, match, images, after)


def image_kernel(scale, at_ref, stat_in, match_in, image_ref, t0, t1, t2, t3, e_ref, a_ref, b_ref, c_ref, d_ref, down_ref, stat_ref, match_ref, own, four, row_by, match_by, weights, sems):
    texts = (t0, t1, t2, t3)
    blocks, _, per, width = image_ref.shape
    cols = t0.shape[0]
    rows = blocks * per
    every = match_in.shape[1]
    place, z, core, first = at_ref[0], at_ref[5], at_ref[6], at_ref[7]
    one, two = 1 + core, 2 - core
    order = [z ^ 3, z ^ 4, z ^ one, z ^ one ^ 7, z ^ two, z ^ two ^ 7, z ^ 7, z]
    fetch = [
        pltpu.make_async_copy(stat_in, stat_ref, sems.at[5]),
        pltpu.make_async_copy(match_in, match_ref, sems.at[6]),
    ]
    fetch += [
        pltpu.make_async_copy(image_ref.at[block, place], own.at[k], sems.at[4]) for k, block in enumerate(order)
    ]
    fetch += [
        pltpu.make_async_copy(texts[k], four.at[pl.ds(k * cols, cols)], sems.at[k]) for k in range(4)
    ]
    for copy in fetch:
        copy.start()
    fetch[0].wait()
    fetch[1].wait()
    row_all = log2_sum(stat_ref[:, 0, :every], 0)
    pair = lax.broadcasted_iota(jnp.int32, (2 * per, 1), 0)
    lane = pair + jnp.where(pair < per, 0, 3 * per) + place * per
    wanted = lax.broadcasted_iota(jnp.int32, (2 * per, 8 * per), 1) == lane
    for k, j in enumerate(range(0, every, 8 * per)):
        window = slice(j, j + 8 * per)
        row = jnp.sum(jnp.where(wanted, row_all[:, window], 0.0), axis=1, keepdims=True)
        match = jnp.sum(jnp.where(wanted, match_ref[:, window], 0), axis=1, keepdims=True)
        row_by[2 * k : 2 * k + 2] = row.reshape(2, per, 1)
        match_by[2 * k : 2 * k + 2] = match.reshape(2, per, 1)
    row = jnp.concatenate([row_by[block] for block in order], axis=0)
    match = jnp.concatenate([match_by[block] for block in order], axis=0)
    ids = lax.broadcasted_iota(jnp.int32, (rows, cols), 1)
    for copy in fetch[2:10]:
        copy.wait()
    mine = own[...].reshape(rows, width)
    for group in ((0,), (1, 2, 3)):
        for k in group:
            fetch[10 + k].wait()
        for k in group:
            where = slice(k * cols, (k + 1) * cols)
            logits = nt_dot(mine, four[where]) * scale
            col = stat_ref[first + (place ^ k), :, every + LANES :]
            weights[:, where] = weigh(logits, row, col, match - at_ref[1 + k] == ids)
    peak = jnp.max(stat_ref[:, 0, every : every + LANES], axis=0, keepdims=True)
    down_ref[...] = down_scale(peak)
    part = jnp.dot(weights[...], four[...], preferred_element_type=F32) * up_scale(peak[:, :1])
    e_ref[...] = part[: 2 * per].astype(e_ref.dtype).reshape(e_ref.shape)
    a_ref[...] = part[2 * per : 4 * per].astype(a_ref.dtype).reshape(a_ref.shape)
    b_ref[...] = part[4 * per : 6 * per].reshape(b_ref.shape)
    c_ref[...] = part[6 * per : 7 * per]
    d_ref[...] = part[7 * per :]


def image_call(at, stats, match, images, texts, scale):
    rows, width = images.shape
    cols = texts[0].shape[0]
    own = rows // 4
    per = rows // 32
    outs = [(2, per, width), (2, per, width), (2, per, width), (per, width), (per, width), (1, LANES)]
    kinds = [BF16, BF16, F32, F32, F32, F32]
    return pl.pallas_call(
        functools.partial(image_kernel, scale),
        in_specs=[SCALARS, ANY, ANY] + [HBM] * 5,
        out_specs=[VMEM] * 6,
        out_shape=[jax.ShapeDtypeStruct(s, t) for s, t in zip(outs, kinds)],
        scratch_shapes=[
            pltpu.VMEM(stats.shape, F32),
            pltpu.VMEM(match.shape, jnp.int32),
            pltpu.VMEM((8, per, width), BF16),
            pltpu.VMEM((4 * cols, width), BF16),
            pltpu.VMEM((8, per, 1), F32),
            pltpu.VMEM((8, per, 1), jnp.int32),
            pltpu.VMEM((own, 4 * cols), BF16),
            pltpu.SemaphoreType.DMA((7,)),
        ],
        compiler_params=params(50),
        cost_estimate=FREE,
        name="image_part",
    )(at, stats, match, images.reshape(8, 4, per, width), *texts)


def shards(images, texts, match):
    rows, width = images.shape
    cols = texts.shape[0]
    scale = 2.0 / math.sqrt(width) * LOG2E
    zhi, zb, za, yhi, core = (lax.axis_index(a) for a in TXT)
    place = yhi * 2 + core
    z = zhi * 4 + zb * 2 + za

    other_yhi = swap(texts, "yhi")
    other_core = swap(texts, "core")

    logits, row, col = first_call(texts, images, scale)
    cross = z_swap(row, (7, 7))
    row = merge(row, cross, rows)
    near = z_swap(row, (1, 1))
    got = exchange(col, IMG)
    sent = merge_call(got, row, near)
    other_yhi, sent = tie(other_yhi, sent)
    stats = exchange(sent, ("zb", "yhi", "core"))
    other_both = swap(other_yhi, "core")

    bases = [(z * 4 + (place ^ k)) * cols for k in range(4)]
    at = jnp.stack([place, *bases, z, core, zb * 4])
    match = match[None]
    e, a, b, c, d, down = image_call(at, stats, match, images, (texts, other_core, other_yhi, other_both), scale)
    text_parts = text_call(at, logits, stats, match, images, down)

    e = z_swap(e, (1, 2))
    a = z_swap(a, (1, 2))
    e, text_parts = tie(e, text_parts)
    b = (b + e.astype(F32)).astype(F16)
    b, down = tie(b, down)
    b = z_swap(b, (2, 1))
    down = swap(down, "core")
    down, text_parts = tie(down, text_parts)
    c = c + a[1].astype(F32)
    d = d + a[0].astype(F32)
    text_parts = exchange(text_parts, IMG)
    b, c, d = tie(b, c, d)
    c = z_swap((c + b[1].astype(F32)).astype(F16), (7, 7))
    d = d + b[0].astype(F32)
    text_grad = jnp.sum(text_parts.astype(F32), axis=0)
    c, d = tie(c, d)
    return (d + c.astype(F32)) * down[:, :1], text_grad


def solution(mesh):
    fine = Mesh(mesh.devices.reshape(SIZES), AXES)
    in_specs = (P(IMG, None), P(TXT, None), P(IMG))
    out_specs = (P(IMG + TXT, None), P(TXT + IMG, None))
    return jax.shard_map(shards, mesh=fine, in_specs=in_specs, out_specs=out_specs, check_vma=False)
```

```python
import functools
import math

import jax
import jax.numpy as jnp
from jax import lax
from jax.experimental import pallas as pl
from jax.experimental.pallas import tpu as pltpu
from jax.sharding import Mesh, PartitionSpec as P

AXES = ("ylo", "x", "zhi", "zb", "za", "yhi", "core")
SIZES = (2, 4, 2, 2, 2, 2, 2)
IMG = ("ylo", "x")
TXT = ("zhi", "zb", "za", "yhi", "core")
F32 = jnp.float32
BF16 = jnp.bfloat16
F16 = jnp.float16
LOG2E = 1.4426950408889634
HBM = pl.BlockSpec(memory_space=pltpu.HBM)
ANY = pl.BlockSpec(memory_space=pl.ANY)
VMEM = pl.BlockSpec(memory_space=pltpu.VMEM)
SCALARS = pl.BlockSpec(memory_space=pltpu.SMEM)
FREE = pl.CostEstimate(flops=0, bytes_accessed=0, transcendentals=0)
LANES = 128
MIB = 1024 * 1024


def swap(value, axis):
    return lax.ppermute(value, axis, [(0, 1), (1, 0)])


def z_swap(value, bits):
    pairs = [(z * 2 + c, (z ^ bits[c]) * 2 + c) for z in range(8) for c in range(2)]
    return lax.ppermute(value, ("zhi", "zb", "za", "core"), pairs)


def exchange(copies, axes):
    return lax.all_to_all(copies, axes, 0, 0, tiled=True)


def tie(*values):
    return lax.optimization_barrier(values)


def log2_sum(values, axis):
    top = jnp.max(values, axis=axis, keepdims=True)
    return top + jnp.log2(jnp.sum(jnp.exp2(values - top), axis=axis, keepdims=True))


def merge(own, got, n):
    top = jnp.maximum(own, got)
    total = top + jnp.log2(jnp.exp2(own - top) + jnp.exp2(got - top))
    lanes = lax.broadcasted_iota(jnp.int32, own.shape, 1)
    return jnp.where(lanes < n, total, top)


def params(mib):
    return pltpu.CompilerParams(vmem_limit_bytes=mib * MIB)


def nt_dot(a, b):
    return lax.dot_general(a, b, (((1,), (1,)), ((), ())), preferred_element_type=F32)


def largest(block):
    peak = jnp.max(jnp.abs(block).astype(F32), axis=0, keepdims=True)
    return jnp.max(peak, axis=1, keepdims=True)


def first_kernel(scale, text_in, image_in, logits_out, row_ref, col_ref, text_ref, image_ref, logits_ref, sems):
    cols = text_in.shape[0]
    rows = image_in.shape[0]
    size = rows // 3
    steps = range(0, rows, size)
    fetch = [pltpu.make_async_copy(text_in, text_ref, sems.at[0])]
    fetch += [
        pltpu.make_async_copy(image_in.at[pl.ds(j, size)], image_ref.at[pl.ds(j, size)], sems.at[1 + k])
        for k, j in enumerate(steps)
    ]
    for copy in fetch:
        copy.start()
    fetch[0].wait()
    text = text_ref[...]
    row_ref[:, rows:] = jnp.broadcast_to(largest(text), (1, LANES))
    high = total = None
    store = []
    for k in range(len(steps) + 1):
        if k < len(steps):
            fetch[1 + k].wait()
            where = pl.ds(steps[k], size)
            logits_ref[:, where] = nt_dot(text, image_ref[where]) * scale
            store.append(pltpu.make_async_copy(logits_ref.at[:, where], logits_out.at[:, where], sems.at[4 + k]))
            store[k].start()
        if k == 0:
            continue
        j = steps[k - 1]
        logits = logits_ref[:, j : j + size]
        deep = logits.reshape(cols // 8, 8, size)
        top = jnp.max(deep, axis=0)
        part = jnp.sum(jnp.exp2(deep - top[None]), axis=0)
        best = jnp.max(top, axis=0, keepdims=True)
        part = jnp.sum(part * jnp.exp2(top - best), axis=0, keepdims=True)
        row_ref[:, j : j + size] = best + jnp.log2(part)
        tiles = [logits[:, i : i + LANES] for i in range(0, size, LANES)]
        new = functools.reduce(jnp.maximum, tiles if high is None else [high, *tiles])
        sums = [jnp.exp2(tile - new) for tile in tiles]
        total = functools.reduce(jnp.add, sums if high is None else [total * jnp.exp2(high - new), *sums])
        high = new
    best = jnp.max(high, axis=1, keepdims=True)
    share = best + jnp.log2(jnp.sum(total * jnp.exp2(high - best), axis=1, keepdims=True))
    share = jnp.transpose(jnp.broadcast_to(share, (cols, LANES)))[:1]
    for k in range(col_ref.shape[0]):
        col_ref[k] = share
    for copy in store:
        copy.wait()


def first_call(texts, images, scale):
    cols = texts.shape[0]
    rows = images.shape[0]
    outs = [(cols, rows), (1, rows + LANES), (8, 1, cols)]
    return pl.pallas_call(
        functools.partial(first_kernel, scale),
        in_specs=[HBM] * 2,
        out_specs=[HBM, VMEM, VMEM],
        out_shape=[jax.ShapeDtypeStruct(s, F32) for s in outs],
        scratch_shapes=[
            pltpu.VMEM(texts.shape, BF16),
            pltpu.VMEM(images.shape, BF16),
            pltpu.VMEM((cols, rows), F32),
            pltpu.SemaphoreType.DMA((7,)),
        ],
        compiler_params=params(60),
        cost_estimate=FREE,
        name="logits",
    )(texts, images)


def merge_kernel(got_ref, row_ref, near_ref, out_ref):
    rows = row_ref.shape[1]
    col = log2_sum(got_ref[:, 0, :], 0)
    both = merge(row_ref[...], near_ref[...], rows - LANES)
    for k in range(out_ref.shape[0]):
        out_ref[k, :, :rows] = both
        out_ref[k, :, rows:] = col


def merge_call(got, row, near):
    cols = got.shape[2]
    return pl.pallas_call(
        merge_kernel,
        in_specs=[VMEM] * 3,
        out_specs=VMEM,
        out_shape=jax.ShapeDtypeStruct((8, 1, row.shape[1] + cols), F32),
        compiler_params=params(4),
        cost_estimate=FREE,
        name="merge",
    )(got, row, near)


def weigh(logits, row, col, paired):
    total = jnp.exp2(logits - row) + jnp.exp2(logits - col)
    return (0.5 * total - paired.astype(F32)).astype(BF16)


def up_scale(peak):
    return 8.0 / jnp.maximum(peak, 1e-30)


def down_scale(peak):
    return jnp.maximum(peak, 1e-30) * 0.125


def text_kernel(at_ref, logits_in, stat_in, match_in, image_in, after_ref, out_ref, stat_ref, match_ref, logits_ref, image_ref, weights, sems):
    cols, rows = logits_in.shape
    size = rows // 4
    steps = range(0, rows, size)
    fetch = [
        pltpu.make_async_copy(logits_in.at[:, pl.ds(j, size)], logits_ref.at[:, pl.ds(j, size)], sems.at[k])
        for k, j in enumerate(steps)
    ]
    fetch.append(pltpu.make_async_copy(image_in, image_ref, sems.at[4]))
    facts = [pltpu.make_async_copy(stat_in, stat_ref, sems.at[5]), pltpu.make_async_copy(match_in, match_ref, sems.at[6])]
    for copy in facts + fetch:
        copy.start()
    for copy in facts:
        copy.wait()
    row = log2_sum(stat_ref[:, 0, :rows], 0)
    col = stat_ref[at_ref[7] + at_ref[0], :, rows + LANES :]
    col = jnp.transpose(jnp.broadcast_to(col, (LANES, cols)))[:, :1]
    ids = at_ref[1] + lax.broadcasted_iota(jnp.int32, (cols, size), 0)
    for k, j in enumerate(steps):
        fetch[k].wait()
        paired = match_ref[:, j : j + size] == ids
        weights[:, j : j + size] = weigh(logits_ref[:, j : j + size], row[:, j : j + size], col, paired)
    fetch[4].wait()
    part = jnp.dot(weights[...], image_ref[...], preferred_element_type=F32)
    out_ref[...] = part.astype(BF16).reshape(out_ref.shape)


def text_call(at, logits, stats, match, images, after):
    cols, rows = logits.shape
    width = images.shape[1]
    return pl.pallas_call(
        text_kernel,
        in_specs=[SCALARS, HBM, ANY, ANY, HBM, ANY],
        out_specs=VMEM,
        out_shape=jax.ShapeDtypeStruct((8, cols // 8, width), BF16),
        scratch_shapes=[
            pltpu.VMEM(stats.shape, F32),
            pltpu.VMEM(match.shape, jnp.int32),
            pltpu.VMEM((cols, rows), F32),
            pltpu.VMEM(images.shape, BF16),
            pltpu.VMEM((cols, rows), BF16),
            pltpu.SemaphoreType.DMA((7,)),
        ],
        compiler_params=params(50),
        cost_estimate=FREE,
        name="text_part",
    )(at, logits, stats, match, images, after)


def image_kernel(scale, at_ref, stat_in, match_in, image_ref, t0, t1, t2, t3, e_ref, a_ref, b_ref, c_ref, d_ref, down_ref, stat_ref, match_ref, own, four, row_by, match_by, weights, sems):
    texts = (t0, t1, t2, t3)
    blocks, _, per, width = image_ref.shape
    cols = t0.shape[0]
    rows = blocks * per
    every = match_in.shape[1]
    place, z, core, first = at_ref[0], at_ref[5], at_ref[6], at_ref[7]
    one, two = 1 + core, 2 - core
    order = [z ^ 3, z ^ 5, z ^ one, z ^ one ^ 6, z ^ two, z ^ two ^ 6, z ^ 6, z]
    fetch = [
        pltpu.make_async_copy(stat_in, stat_ref, sems.at[5]),
        pltpu.make_async_copy(match_in, match_ref, sems.at[6]),
    ]
    fetch += [
        pltpu.make_async_copy(image_ref.at[block, place], own.at[k], sems.at[4]) for k, block in enumerate(order)
    ]
    fetch += [
        pltpu.make_async_copy(texts[k], four.at[pl.ds(k * cols, cols)], sems.at[k]) for k in range(4)
    ]
    for copy in fetch:
        copy.start()
    fetch[0].wait()
    fetch[1].wait()
    row_all = log2_sum(stat_ref[:, 0, :every], 0)
    pair = lax.broadcasted_iota(jnp.int32, (2 * per, 1), 0)
    lane = pair + jnp.where(pair < per, 0, 3 * per) + place * per
    wanted = lax.broadcasted_iota(jnp.int32, (2 * per, 8 * per), 1) == lane
    for k, j in enumerate(range(0, every, 8 * per)):
        window = slice(j, j + 8 * per)
        row = jnp.sum(jnp.where(wanted, row_all[:, window], 0.0), axis=1, keepdims=True)
        match = jnp.sum(jnp.where(wanted, match_ref[:, window], 0), axis=1, keepdims=True)
        row_by[2 * k : 2 * k + 2] = row.reshape(2, per, 1)
        match_by[2 * k : 2 * k + 2] = match.reshape(2, per, 1)
    row = jnp.concatenate([row_by[block] for block in order], axis=0)
    match = jnp.concatenate([match_by[block] for block in order], axis=0)
    ids = lax.broadcasted_iota(jnp.int32, (rows, cols), 1)
    for copy in fetch[2:10]:
        copy.wait()
    mine = own[...].reshape(rows, width)
    for group in ((0,), (1, 2, 3)):
        for k in group:
            fetch[10 + k].wait()
        for k in group:
            where = slice(k * cols, (k + 1) * cols)
            logits = nt_dot(mine, four[where]) * scale
            col = stat_ref[first + (place ^ k), :, every + LANES :]
            weights[:, where] = weigh(logits, row, col, match - at_ref[1 + k] == ids)
    peak = jnp.max(stat_ref[:, 0, every : every + LANES], axis=0, keepdims=True)
    down_ref[...] = down_scale(peak)
    part = jnp.dot(weights[...], four[...], preferred_element_type=F32) * up_scale(peak[:, :1])
    e_ref[...] = part[: 2 * per].astype(e_ref.dtype).reshape(e_ref.shape)
    a_ref[...] = part[2 * per : 4 * per].astype(a_ref.dtype).reshape(a_ref.shape)
    b_ref[...] = part[4 * per : 6 * per].reshape(b_ref.shape)
    c_ref[...] = part[6 * per : 7 * per]
    d_ref[...] = part[7 * per :]


def image_call(at, stats, match, images, texts, scale):
    rows, width = images.shape
    cols = texts[0].shape[0]
    own = rows // 4
    per = rows // 32
    outs = [(2, per, width), (2, per, width), (2, per, width), (per, width), (per, width), (1, LANES)]
    kinds = [BF16, BF16, F32, F32, F32, F32]
    return pl.pallas_call(
        functools.partial(image_kernel, scale),
        in_specs=[SCALARS, ANY, ANY] + [HBM] * 5,
        out_specs=[VMEM] * 6,
        out_shape=[jax.ShapeDtypeStruct(s, t) for s, t in zip(outs, kinds)],
        scratch_shapes=[
            pltpu.VMEM(stats.shape, F32),
            pltpu.VMEM(match.shape, jnp.int32),
            pltpu.VMEM((8, per, width), BF16),
            pltpu.VMEM((4 * cols, width), BF16),
            pltpu.VMEM((8, per, 1), F32),
            pltpu.VMEM((8, per, 1), jnp.int32),
            pltpu.VMEM((own, 4 * cols), BF16),
            pltpu.SemaphoreType.DMA((7,)),
        ],
        compiler_params=params(50),
        cost_estimate=FREE,
        name="image_part",
    )(at, stats, match, images.reshape(8, 4, per, width), *texts)


def shards(images, texts, match):
    rows, width = images.shape
    cols = texts.shape[0]
    scale = 2.0 / math.sqrt(width) * LOG2E
    zhi, zb, za, yhi, core = (lax.axis_index(a) for a in TXT)
    place = yhi * 2 + core
    z = zhi * 4 + zb * 2 + za

    other_yhi = swap(texts, "yhi")
    other_core = swap(texts, "core")

    logits, row, col = first_call(texts, images, scale)
    cross = z_swap(row, (6, 6))
    row = merge(row, cross, rows)
    near = z_swap(row, (1, 1))
    got = exchange(col, IMG)
    sent = merge_call(got, row, near)
    other_yhi, sent = tie(other_yhi, sent)
    stats = exchange(sent, ("zb", "yhi", "core"))
    other_both = swap(other_yhi, "core")

    bases = [(z * 4 + (place ^ k)) * cols for k in range(4)]
    at = jnp.stack([place, *bases, z, core, zb * 4])
    match = match[None]
    e, a, b, c, d, down = image_call(at, stats, match, images, (texts, other_core, other_yhi, other_both), scale)
    text_parts = text_call(at, logits, stats, match, images, down)

    e = z_swap(e, (1, 2))
    a = z_swap(a, (1, 2))
    e, text_parts = tie(e, text_parts)
    b = (b + e.astype(F32)).astype(F16)
    b, down = tie(b, down)
    b = z_swap(b, (2, 1))
    down = swap(down, "core")
    down, text_parts = tie(down, text_parts)
    c = c + a[1].astype(F32)
    d = d + a[0].astype(F32)
    text_parts = exchange(text_parts, IMG)
    b, c, d = tie(b, c, d)
    c = z_swap((c + b[1].astype(F32)).astype(F16), (6, 6))
    d = d + b[0].astype(F32)
    text_grad = jnp.sum(text_parts.astype(F32), axis=0)
    c, d = tie(c, d)
    return (d + c.astype(F32)) * down[:, :1], text_grad


def solution(mesh):
    fine = Mesh(mesh.devices.reshape(SIZES), AXES)
    in_specs = (P(IMG, None), P(TXT, None), P(IMG))
    out_specs = (P(IMG + TXT, None), P(TXT + IMG, None))
    return jax.shard_map(shards, mesh=fine, in_specs=in_specs, out_specs=out_specs, check_vma=False)
```
